512 devices in a mesh: rows: 64 (over y, z), cols: 8 (over x, core).
Axes of the slice: x: 4, y: 8, z: 8, core: 2. Of those that a mesh axis runs over, the one named last changes fastest.
Arguments:
- node_feats: bfloat16 [65536, 128], P(('rows', 'cols')), may hold values from -6 to 6
- weight: bfloat16 [128, 256], replicated, may hold values from -0.5 to 0.5
- att_src: float32 [256], replicated, may hold values from -1.2 to 1.2
- att_dst: float32 [256], replicated, may hold values from -1.2 to 1.2
- out_bias: float32 [256], replicated, may hold values from -3 to 3
- block_src: int32 [512, 8, 32], P(('rows', 'cols')), may hold values from 0 to 63, as said below
- block_count: int32 [512, 8], P(('rows', 'cols')), may hold values from 4 to 32, as said below
- block_bits: int32 [512, 8, 32, 16, 128], P(('rows', 'cols')), may hold values from 0 to 255, as said below
Outputs:
- gat_out: bfloat16 [65536, 256], P(('rows', 'cols'))
The draws below stay inside these ranges and needn't reach their ends.
Inputs may be any that keep to these rules, and one draw needn't show every extreme that they name: `block_src`: within one block row of one list the 32 slots name distinct source blocks. `block_count`: each entry is 4, 8, 16 or 32; some block row holds 32 in every draw. `block_bits`: each word holds 8 adjacency bits, bit k of word w standing for source column 8 w + k of the block.
All inputs are finite; a program needn't handle non-finite values.
Results may differ from the reference program's by a relative error of at most 0.01.
Values may be sent and summed in bfloat16 or wider, within the bound.
A program may use at most 64 MiB of HBM per device.

```python
import jax
import jax.numpy as jnp
from jax import lax

HID = 256
HEADS = 4
F_IN = 128
BLOCK = 128
NODE_DEV = 128
HEAD_DIM = 64
DEST_BLK = 8
SRC_BLK = 64
ROW_LINKS = 32
WORDS = 16
NODES = 65536
N_ROWS = 64
N_COLS = 8


def draw_block_src(key, part):
    key = jax.random.fold_in(key, 3)
    row_total = N_ROWS * N_COLS * DEST_BLK
    row_keys = jax.random.split(key, row_total)

    def one_order(row_key):
        return jax.random.permutation(row_key, SRC_BLK)
    orderings = jax.vmap(one_order)(row_keys)
    return orderings[:, :ROW_LINKS].reshape(N_ROWS * N_COLS, DEST_BLK, ROW_LINKS).astype(jnp.int32)


def draw_block_count(key, part):
    key = jax.random.fold_in(key, 5)
    level_key, full_key = jax.random.split(key)
    row_total = N_ROWS * N_COLS * DEST_BLK
    levels = jax.random.randint(level_key, (row_total,), 0, 4)
    counts = jnp.left_shift(jnp.full((row_total,), ROW_LINKS // 8, jnp.int32), levels.astype(jnp.int32))
    chosen = jax.random.randint(full_key, (), 0, row_total)
    position = jnp.arange(row_total, dtype=jnp.int32)
    flattened = jnp.where(position == chosen, ROW_LINKS, counts)
    return flattened.reshape(N_ROWS * N_COLS, DEST_BLK).astype(jnp.int32)


def draw_block_bits(key, part):
    key = jax.random.fold_in(key, 7)
    row_total = N_ROWS * N_COLS * DEST_BLK
    row_keys = jax.random.split(key, row_total)
    powers = jnp.left_shift(jnp.ones((8,), jnp.int32), jnp.arange(8, dtype=jnp.int32))

    def one_row(row_key):
        uniform_draws = jax.random.randint(row_key, (ROW_LINKS, BLOCK // 8, 8, BLOCK), 0, 50)
        edge_bits = (uniform_draws == 0).astype(jnp.int32)
        return jnp.sum(edge_bits * powers[None, None, :, None], axis=2)
    packed = lax.map(one_row, row_keys)
    return packed.reshape(N_ROWS * N_COLS, DEST_BLK, ROW_LINKS, BLOCK // 8, BLOCK).astype(jnp.int32)


def block_scale(own_key, shape, cuts, smallest, largest):
    factor_of, own = 1.0, jax.random.fold_in(own_key, 6)
    for dim, blocks in cuts:
        draws = jnp.exp(jax.random.uniform(jax.random.fold_in(own, dim), (blocks,), jnp.float32, smallest / len(cuts), largest / len(cuts)))
        factor_of = factor_of * jnp.repeat(draws, shape[dim] // blocks).reshape([-1 if axis == dim else 1 for axis in range(len(shape))])
    return factor_of


def scatter_about(key, dims, spread, most, cuts=(), held_as=jnp.bfloat16):
    gain = block_scale(key, dims, cuts, -0.22, 0.18) if cuts else 1.0
    result = jax.random.normal(key, dims, jnp.float32) * spread * gain
    return jnp.minimum(jnp.maximum(result, -most), most).astype(held_as)


def setup_inputs(seed: int = 0) -> dict:
    key_of = jax.random.split(jax.random.key(seed), 9)
    node_feats = scatter_about(key_of[0], (NODES, F_IN), 1.0, 6.0, ((0, 512),))
    weight = scatter_about(key_of[1], (F_IN, HID), F_IN ** -0.5, 0.5)
    att_src = scatter_about(key_of[2], (HID,), 0.2, 1.2, (), jnp.float32)
    att_dst = scatter_about(key_of[3], (HID,), 0.2, 1.2, (), jnp.float32)
    out_bias = scatter_about(key_of[4], (HID,), 0.5, 3.0, (), jnp.float32)
    block_src = draw_block_src(jax.random.fold_in(key_of[8], 71), 0)
    block_count = draw_block_count(jax.random.fold_in(key_of[8], 71), 0)
    block_bits = draw_block_bits(jax.random.fold_in(key_of[8], 71), 0)
    return dict(node_feats=node_feats, weight=weight, att_src=att_src, att_dst=att_dst, out_bias=out_bias, block_src=block_src, block_count=block_count, block_bits=block_bits)


SLOPE = 0.2


def leaky_relu(raw_score):
    return jnp.where(raw_score > 0, raw_score, SLOPE * raw_score)


def head_scores(projected, attention):
    scaled = projected.astype(jnp.float32) * attention[None, :]
    return jnp.sum(scaled.reshape(projected.shape[0], HEADS, HEAD_DIM), axis=2).T


def unpack_bits(packed):
    shifts = jnp.arange(8, dtype=jnp.int32)
    expanded = jnp.right_shift(packed[..., :, None, :], shifts[:, None]) & 1
    new_shape = packed.shape[:-2] + (packed.shape[-2] * 8, packed.shape[-1])
    return expanded.reshape(new_shape).astype(jnp.float32)


def reference(node_feats, weight, att_src, att_dst, out_bias, block_src, block_count, block_bits):
    projected = jnp.dot(node_feats, weight, preferred_element_type=jnp.float32).astype(jnp.bfloat16)
    source_scores = head_scores(projected, att_src)
    target_scores = head_scores(projected, att_dst)
    list_total = N_ROWS * N_COLS
    list_index = jnp.arange(list_total, dtype=jnp.int32)
    row_of = list_index // N_COLS
    col_of = list_index % N_COLS
    per_shard = NODE_DEV // BLOCK
    block_total = NODES // BLOCK
    dest_global = (row_of[:, None] * DEST_BLK + jnp.arange(DEST_BLK, dtype=jnp.int32)[None, :]).reshape(-1)
    src_global = ((block_src // per_shard) * N_COLS + col_of[:, None, None]) * per_shard + block_src % per_shard
    src_global = src_global.reshape(-1, ROW_LINKS).astype(jnp.int32)
    alive = (jnp.arange(ROW_LINKS, dtype=jnp.int32)[None, None, :] < block_count[:, :, None]).reshape(-1, ROW_LINKS)
    packed = block_bits.reshape(-1, ROW_LINKS, WORDS, BLOCK)
    values = projected.reshape(block_total, BLOCK, HEADS, HEAD_DIM)
    source_blocks = source_scores.reshape(HEADS, block_total, BLOCK)
    target_blocks = target_scores.reshape(HEADS, block_total, BLOCK)

    def one_row(running, inputs):
        numerator, denominator = running
        dest_block, sources, alive_slots, edge_bits = inputs
        edge_mask = unpack_bits(edge_bits) * alive_slots.astype(jnp.float32)[:, None, None]
        target = target_blocks[:, dest_block]
        source = source_blocks[:, sources].transpose(1, 0, 2)
        raw_score = target[None, :, None, :] + source[:, :, :, None]
        rounded = (jnp.exp(leaky_relu(raw_score)) * edge_mask[:, None]).astype(jnp.bfloat16)
        weights = lax.optimization_barrier(rounded).astype(jnp.float32)
        contrib = jnp.einsum("lhji,ljhk->ihk", weights, values[sources].astype(jnp.float32))
        numerator = numerator.at[dest_block].add(contrib)
        denominator = denominator.at[:, dest_block].add(jnp.sum(weights, axis=(0, 2)))
        return (numerator, denominator), None

    initial = (jnp.zeros((block_total, BLOCK, HEADS, HEAD_DIM), jnp.float32),
               jnp.zeros((HEADS, block_total, BLOCK), jnp.float32))
    (numerator, denominator), unused = lax.scan(one_row, initial, (dest_global, src_global, alive, packed))
    numerator = numerator.reshape(NODES, HEADS, HEAD_DIM)
    denominator = denominator.reshape(HEADS, NODES).T
    self_round = jnp.exp(leaky_relu(target_scores + source_scores)).astype(jnp.bfloat16)
    self_weight = lax.optimization_barrier(self_round).astype(jnp.float32).T
    numerator = numerator + self_weight[:, :, None] * projected.astype(jnp.float32).reshape(NODES, HEADS, HEAD_DIM)
    denominator = denominator + self_weight
    blended = (numerator / denominator[:, :, None]).reshape(NODES, HID)
    return jax.nn.elu(blended + out_bias[None, :]).astype(jnp.bfloat16)
```

```python
import functools
import math

import jax
import jax.numpy as jnp
from jax import lax
from jax.experimental import pallas as pl
from jax.experimental.pallas import tpu as pltpu
from jax.sharding import PartitionSpec as P

HEADS = 4
BLOCK = 128
HEAD_DIM = 64
HID = HEADS * HEAD_DIM
HALF = BLOCK // 2
SLOPE = 0.2
RISE = 1.0 - SLOPE
SAFE = 100.0
V_ROWS = 80
P_ROWS = HID + 16
GROUP = 4
MESH = pl.DeviceIdType.MESH
F32 = jnp.float32
BF16 = jnp.bfloat16
NT = (((1,), (1,)), ((), ()))
TN = (((0,), (0,)), ((), ()))


def leaky_relu(raw):
    return jnp.where(raw > 0, raw, SLOPE * raw)


def attention_rows(att):
    high = att.astype(BF16).astype(F32)
    middle = (att - high).astype(BF16).astype(F32)
    low = att - high - middle
    row = lax.broadcasted_iota(jnp.int32, (32, HID), 0)
    column = lax.broadcasted_iota(jnp.int32, (32, HID), 1)
    piece = jnp.where(row < 8, high, jnp.where(row < 16, middle, low))
    return jnp.where((row % 8 == column // HEAD_DIM) & (row < 24), piece, 0.0).astype(BF16)


def scores_of(rows, projected_t):
    parts = jnp.dot(rows, projected_t, preferred_element_type=F32)
    return parts[0:8] + parts[8:16] + parts[16:24]


def project_t(weight_t, feats):
    return lax.dot_general(weight_t, feats, NT, preferred_element_type=F32).astype(BF16)


def transposed(weight):
    return jnp.transpose(weight.astype(F32)).astype(BF16)


def gather_kernel(side, cols, x_ref, w_ref, adst_ref, ga_ref, gb_ref, d_ref, xp, dme,
                  local_sem, d_send, d_recv, one_send, one_recv, two_send, two_recv):
    r, c = lax.axis_index("rows"), lax.axis_index("cols")
    y, z = r // side, r % side

    def at(yy, zz):
        return (yy * side + zz, c)

    barrier = pltpu.get_barrier_semaphore()
    for k in range(1, side):
        pl.semaphore_signal(barrier, inc=1, device_id=at(y, (z + k) % side), device_id_type=MESH)
        pl.semaphore_signal(barrier, inc=1, device_id=at((y + k) % side, z), device_id_type=MESH)
    for k in range(1, cols):
        pl.semaphore_signal(barrier, inc=1, device_id=(r, (c + k) % cols), device_id_type=MESH)

    place = lax.broadcasted_iota(jnp.int32, (BLOCK, BLOCK), 0)
    node = lax.broadcasted_iota(jnp.int32, (BLOCK, BLOCK), 1)
    order = jnp.where(node == 8 * (place % 16) + place // 16, 1.0, 0.0).astype(BF16)
    xp[...] = jnp.dot(order, x_ref[...], preferred_element_type=F32).astype(BF16)
    dme[...] = scores_of(attention_rows(adst_ref[...]), project_t(transposed(w_ref[...]), x_ref[...]))
    pl.semaphore_wait(barrier, 2 * (side - 1) + cols - 1)

    first = []
    for k in range(1, side):
        first.append(pltpu.make_async_remote_copy(
            xp.at[pl.ds(0, HALF)], ga_ref.at[y, z], one_send.at[0, k - 1], one_recv.at[0, k - 1],
            device_id=at(y, (z + k) % side), device_id_type=MESH))
        first.append(pltpu.make_async_remote_copy(
            xp.at[pl.ds(HALF, HALF)], gb_ref.at[z, y], one_send.at[1, k - 1], one_recv.at[1, k - 1],
            device_id=at((y + k) % side, z), device_id_type=MESH))
    for copy in first:
        copy.start()
    own = [
        pltpu.make_async_copy(xp.at[pl.ds(0, HALF)], ga_ref.at[y, z], local_sem.at[0]),
        pltpu.make_async_copy(xp.at[pl.ds(HALF, HALF)], gb_ref.at[z, y], local_sem.at[1]),
        pltpu.make_async_copy(dme, d_ref.at[c], local_sem.at[2]),
    ]
    for copy in own:
        copy.start()
    scores = []
    for k in range(1, cols):
        scores.append(pltpu.make_async_remote_copy(
            dme, d_ref.at[c], d_send.at[k - 1], d_recv.at[k - 1],
            device_id=(r, (c + k) % cols), device_id_type=MESH))
        scores[-1].start()
    for copy in own:
        copy.wait()
    for copy in first:
        copy.wait_recv()

    sub = side // 2
    half_way = side // 2

    def second(half, way, step, part):
        buffer, place = (ga_ref, y) if half == 0 else (gb_ref, z)
        if way == 0:
            block, target = (place - step + 1 + side) % side, (place + 1) % side
        else:
            block, target = (place + step - 1) % side, (place + side - 1) % side
        ref = buffer.at[block, pl.ds(part * sub, sub)]
        return pltpu.make_async_remote_copy(
            ref, ref, two_send.at[half, way, step - 1, part], two_recv.at[half, way, step - 1, part],
            device_id=at(target, z) if half == 0 else at(y, target), device_id_type=MESH)

    lanes = [(half, way) for half in range(2) for way in range(2)]
    inflight = {}
    for step in range(1, half_way + 1):
        for part in range(2):
            for half, way in lanes:
                if step > 1:
                    inflight[half, way, step - 1, part].wait_recv()
                if step < half_way or part == way:
                    inflight[half, way, step, part] = second(half, way, step, part)
                    inflight[half, way, step, part].start()
    for half, way in lanes:
        inflight[half, way, half_way, way].wait_recv()
    for copy in scores:
        copy.wait_recv()
    for copy in first + scores + list(inflight.values()):
        copy.wait_send()


def gather(side, cols, node_feats, weight, att_dst):
    vmem = pl.BlockSpec(memory_space=pltpu.VMEM)
    hbm = pl.BlockSpec(memory_space=pl.ANY)
    dma = pltpu.SemaphoreType.DMA
    return pl.pallas_call(
        functools.partial(gather_kernel, side, cols),
        out_shape=(
            jax.ShapeDtypeStruct((side, side, HALF, BLOCK), BF16),
            jax.ShapeDtypeStruct((side, side, HALF, BLOCK), BF16),
            jax.ShapeDtypeStruct((cols, 8, BLOCK), F32),
        ),
        in_specs=[vmem, vmem, vmem],
        out_specs=(hbm, hbm, hbm),
        scratch_shapes=[
            pltpu.VMEM((BLOCK, BLOCK), BF16),
            pltpu.VMEM((8, BLOCK), F32),
            dma((3,)), dma((cols - 1,)), dma((cols - 1,)),
            dma((2, side - 1)), dma((2, side - 1)),
            dma((2, 2, side // 2, 2)), dma((2, 2, side // 2, 2)),
        ],
        compiler_params=pltpu.CompilerParams(collective_id=0, has_side_effects=True),
        name="gather_features",
    )(node_feats, weight, att_dst)


def aggregate_kernel(side, src_ref, count_ref, bits_ref, ga_ref, gb_ref, d_ref, w_ref, asrc_ref, p_ref,
                     vt, eb, st, acc):
    dest = d_ref.shape[0]
    weight_t = transposed(w_ref[...])
    rows = attention_rows(asrc_ref[...])
    ones_row = jnp.where(lax.broadcasted_iota(jnp.int32, (16, BLOCK), 0) == 0, 1.0, 0.0)
    spread_row = lax.broadcasted_iota(jnp.int32, (16, HEADS * BLOCK), 0)
    spread_col = lax.broadcasted_iota(jnp.int32, (16, HEADS * BLOCK), 1)
    spread = jnp.where(spread_row == spread_col // BLOCK, 1.0, 0.0).astype(BF16)

    def blocks_of(y):
        pieces = []
        for z in range(side):
            pieces += [ga_ref[y, z], gb_ref[z, y]]
        feats = jnp.concatenate(pieces, axis=0)
        projected = project_t(weight_t, feats)
        return projected, scores_of(rows, projected)

    def prepare(y, largest):
        projected, score = blocks_of(y)
        scale = jnp.exp(SLOPE * score)
        rise = jnp.exp(RISE * score)
        rise = jnp.concatenate([rise, jnp.zeros_like(rise)], axis=0).astype(BF16)
        for z in range(side):
            at = slice(z * BLOCK, (z + 1) * BLOCK)
            block = y * side + z
            for h in range(HEADS):
                c_row = scale[h:h + 1, at]
                values = projected[h * HEAD_DIM:(h + 1) * HEAD_DIM, at].astype(F32) * c_row
                vt[block, h] = jnp.concatenate([values, ones_row * c_row], axis=0).astype(BF16)
            source = lax.dot_general(rise[:, at], spread, TN, preferred_element_type=F32).astype(BF16)
            for h in range(HEADS):
                eb[block, pl.ds(h * BLOCK, BLOCK)] = source[:, h * BLOCK:(h + 1) * BLOCK]
        return jnp.maximum(largest, jnp.abs(score))

    largest = lax.fori_loop(0, side, prepare, jnp.zeros((8, side * BLOCK), F32))
    largest = jnp.maximum(jnp.max(largest), jnp.max(jnp.abs(d_ref[...])))
    safe = largest <= SAFE

    def run(weights_of, finish):
        def one_row(d, carry):
            acc[...] = jnp.zeros_like(acc)
            own = d_ref[d]

            def one_group(g, inner):
                slots = [g * GROUP + i for i in range(GROUP)]
                blocks = [src_ref[d, slot] for slot in slots]
                per_slot = [weights_of(d, slot, block, own) for slot, block in zip(slots, blocks)]
                for h in range(HEADS):
                    edge = jnp.concatenate([piece for one in per_slot for piece in one[h]], axis=0)
                    values = jnp.concatenate([vt[block, h] for block in blocks], axis=1)
                    acc[h] += jnp.dot(values, edge, preferred_element_type=F32)
                return inner

            lax.fori_loop(0, count_ref[d] // GROUP, one_group, 0)
            finish(d, own)
            return carry

        lax.fori_loop(0, dest, one_row, 0)

    def store(d, factor):
        denominators = []
        for h in range(HEADS):
            scaled = acc[h] * factor[h:h + 1, :]
            p_ref[d, pl.ds(h * HEAD_DIM, HEAD_DIM)] = scaled[:HEAD_DIM].astype(BF16)
            denominators.append(scaled[HEAD_DIM:HEAD_DIM + 1])
        denominators.append(jnp.zeros((16 - HEADS, BLOCK), F32))
        p_ref[d, pl.ds(HID, 16)] = jnp.concatenate(denominators, axis=0).astype(BF16)

    def factored(d, slot, block, own):
        words = bits_ref[d, slot].astype(jnp.int16)
        live = [(words & (1 << k)) != 0 for k in range(8)]
        reach = jnp.exp(RISE * own).astype(BF16)
        one = jnp.ones((16, BLOCK), BF16)
        none = jnp.zeros((16, BLOCK), BF16)
        result = []
        for h in range(HEADS):
            target = jnp.broadcast_to(reach[h:h + 1, :], (16, BLOCK))
            pieces = []
            for k in range(8):
                source = eb[block, pl.ds(h * BLOCK + k * 16, 16)]
                pieces.append(jnp.where(live[k], jnp.maximum(source * target, one), none))
            result.append(pieces)
        return result

    @pl.when(safe)
    def _():
        run(factored, lambda d, own: store(d, jnp.exp(SLOPE * own)))

    def direct(d, slot, block, own):
        words = bits_ref[d, slot]
        live = jnp.concatenate([jnp.right_shift(words, k) & 1 for k in range(8)], axis=0) != 0
        result = []
        for h in range(HEADS):
            raw = st[block, :, pl.ds(h, 1)] + own[h:h + 1, :]
            result.append([jnp.where(live, jnp.exp(leaky_relu(raw)), 0.0).astype(BF16)])
        return result

    @pl.when(jnp.logical_not(safe))
    def _():
        def prepare_direct(y, carry):
            projected, score = blocks_of(y)
            for z in range(side):
                at = slice(z * BLOCK, (z + 1) * BLOCK)
                block = y * side + z
                for h in range(HEADS):
                    values = projected[h * HEAD_DIM:(h + 1) * HEAD_DIM, at].astype(F32)
                    vt[block, h] = jnp.concatenate([values, ones_row], axis=0).astype(BF16)
                st[block] = jnp.transpose(score[:, at])
            return carry

        lax.fori_loop(0, side, prepare_direct, 0)
        run(direct, lambda d, own: store(d, jnp.ones_like(own)))


def aggregate(side, block_src, block_count, block_bits, ga, gb, target_scores, weight, att_src):
    vmem = pl.BlockSpec(memory_space=pltpu.VMEM)
    smem = pl.BlockSpec(memory_space=pltpu.SMEM)
    dest = block_src.shape[0]
    sources = side * side
    return pl.pallas_call(
        functools.partial(aggregate_kernel, side),
        out_shape=jax.ShapeDtypeStruct((dest, P_ROWS, BLOCK), BF16),
        in_specs=[smem, smem, vmem, vmem, vmem, vmem, vmem, vmem],
        out_specs=vmem,
        scratch_shapes=[
            pltpu.VMEM((sources, HEADS, V_ROWS, BLOCK), BF16),
            pltpu.VMEM((sources, HEADS * BLOCK, BLOCK), BF16),
            pltpu.VMEM((sources, BLOCK, 8), F32),
            pltpu.VMEM((HEADS, V_ROWS, BLOCK), F32),
        ],
        compiler_params=pltpu.CompilerParams(vmem_limit_bytes=40 * 1024 * 1024),
        name="aggregate_edges",
    )(block_src, block_count, block_bits, ga, gb, target_scores, weight, att_src)


def combine_kernel(cols, p_ref, x_ref, w_ref, asrc_ref, adst_ref, bias_ref, out_ref, land, send, recv):
    r, c = lax.axis_index("rows"), lax.axis_index("cols")
    barrier = pltpu.get_barrier_semaphore()
    for k in range(1, cols):
        pl.semaphore_signal(barrier, inc=1, device_id=(r, (c + k) % cols), device_id_type=MESH)
    pl.semaphore_wait(barrier, cols - 1)
    copies = []
    for k in range(1, cols):
        peer = (c + k) % cols
        copies.append(pltpu.make_async_remote_copy(
            p_ref.at[peer], land.at[k - 1], send.at[k - 1], recv.at[k - 1],
            device_id=(r, peer), device_id_type=MESH))
        copies[-1].start()

    projected = project_t(transposed(w_ref[...]), x_ref[...])
    raw = scores_of(attention_rows(asrc_ref[...]), projected) + scores_of(attention_rows(adst_ref[...]), projected)
    self_weight = jnp.exp(leaky_relu(raw)).astype(BF16).astype(F32)
    own = p_ref[c].astype(F32)
    numerator = [
        own[h * HEAD_DIM:(h + 1) * HEAD_DIM]
        + projected[h * HEAD_DIM:(h + 1) * HEAD_DIM].astype(F32) * self_weight[h:h + 1]
        for h in range(HEADS)
    ]
    total = jnp.concatenate(numerator, axis=0)
    denominator = own[HID:HID + 8] + self_weight
    for k, copy in enumerate(copies):
        copy.wait_recv()
        total = total + land[k, pl.ds(0, HID)].astype(F32)
        denominator = denominator + land[k, pl.ds(HID, 16)].astype(F32)[:8]
    blended = jnp.concatenate(
        [total[h * HEAD_DIM:(h + 1) * HEAD_DIM] / denominator[h:h + 1] for h in range(HEADS)], axis=0)
    value = jnp.transpose(blended) + bias_ref[...]
    out_ref[...] = jnp.where(value > 0, value, jnp.exp(jnp.minimum(value, 0.0)) - 1.0).astype(BF16)
    for copy in copies:
        copy.wait_send()


def combine(cols, partials, node_feats, weight, att_src, att_dst, out_bias):
    vmem = pl.BlockSpec(memory_space=pltpu.VMEM)
    return pl.pallas_call(
        functools.partial(combine_kernel, cols),
        out_shape=jax.ShapeDtypeStruct((BLOCK, HID), BF16),
        in_specs=[vmem] * 6,
        out_specs=vmem,
        scratch_shapes=[
            pltpu.VMEM((cols - 1, P_ROWS, BLOCK), BF16),
            pltpu.SemaphoreType.DMA((cols - 1,)),
            pltpu.SemaphoreType.DMA((cols - 1,)),
        ],
        compiler_params=pltpu.CompilerParams(collective_id=1, has_side_effects=True),
        name="combine_partials",
    )(partials, node_feats, weight, att_src, att_dst, out_bias)


def shards(side, cols, node_feats, weight, att_src, att_dst, out_bias, block_src, block_count, block_bits):
    att_src, att_dst, out_bias = (v.reshape(1, HID) for v in (att_src, att_dst, out_bias))
    ga, gb, target_scores = gather(side, cols, node_feats, weight, att_dst)
    partials = aggregate(
        side, block_src[0], block_count[0], block_bits[0], ga, gb, target_scores, weight, att_src)
    return combine(cols, partials, node_feats, weight, att_src, att_dst, out_bias)


def solution(mesh):
    side = math.isqrt(mesh.shape["rows"])
    cols = mesh.shape["cols"]
    in_specs = (
        P(("rows", "cols"), None),
        P(),
        P(),
        P(),
        P(),
        P(("rows", "cols"), None, None),
        P(("rows", "cols"), None),
        P(("rows", "cols"), None, None, None, None),
    )
    return jax.shard_map(
        functools.partial(shards, side, cols), mesh=mesh, in_specs=in_specs,
        out_specs=P(("rows", "cols"), None), check_vma=False)
```

```python
import functools
import math

import jax
import jax.numpy as jnp
from jax import lax
from jax.experimental import pallas as pl
from jax.experimental.pallas import tpu as pltpu
from jax.sharding import PartitionSpec as P

HEADS = 4
BLOCK = 128
HEAD_DIM = 64
HID = HEADS * HEAD_DIM
SLOPE = 0.2
RISE = 1.0 - SLOPE
SAFE = 100.0
V_ROWS = 80
P_ROWS = HID + 16
OPEN = float(jnp.finfo(jnp.bfloat16).max)
HALF = BLOCK // 2
SUM_ROWS = HID + 16
GROUP = 4
MESH = pl.DeviceIdType.MESH
F32 = jnp.float32
BF16 = jnp.bfloat16
NT = (((1,), (1,)), ((), ()))


def leaky_relu(raw_score):
    return jnp.where(raw_score > 0, raw_score, SLOPE * raw_score)


def attention_rows(att_src, att_dst):
    row = lax.broadcasted_iota(jnp.int32, (32, HID), 0)
    column = lax.broadcasted_iota(jnp.int32, (32, HID), 1)
    att = jnp.where(row % 8 < HEADS, att_src, att_dst)
    high = att.astype(BF16).astype(F32)
    middle = (att - high).astype(BF16).astype(F32)
    low = att - high - middle
    piece = jnp.where(row < 8, high, jnp.where(row < 16, middle, low))
    return jnp.where((row % HEADS == column // HEAD_DIM) & (row < 24), piece, 0.0).astype(BF16)


def scores_of(rows, projected_t):
    parts = jnp.dot(rows, projected_t, preferred_element_type=F32)
    return parts[0:8] + parts[8:16] + parts[16:24]


def project_t(weight_t, feats):
    return lax.dot_general(weight_t, feats, NT, preferred_element_type=F32).astype(BF16)


def layer_kernel(side, cols, src_ref, count_ref, x_any, w_any, asrc_any, adst_any, bias_any, bits_any, out_ref, peak_ref,
                 x_ref, w_ref, asrc_ref, adst_ref, bias_ref, bits, feats, dme, dall, wt, rows, vt, eb, mask, parts, land,
                 own_total, own_weight, load_sem, d_send, d_recv, one_send, one_recv, two_send, two_recv, rs_send, rs_recv):
    r, c = lax.axis_index("rows"), lax.axis_index("cols")
    y, z = r // side, r % side
    quarter = side // 2
    links = bits.shape[1]

    def at(yy, zz):
        return (yy * side + zz, c)

    barrier = pltpu.get_barrier_semaphore()
    for k in range(1, side):
        pl.semaphore_signal(barrier, inc=1, device_id=at(y, (z + k) % side), device_id_type=MESH)
        pl.semaphore_signal(barrier, inc=1, device_id=at((y + k) % side, z), device_id_type=MESH)
    for k in range(1, cols):
        pl.semaphore_signal(barrier, inc=1, device_id=(r, (c + k) % cols), device_id_type=MESH)

    loads = [
        pltpu.make_async_copy(a, b, load_sem.at[i])
        for i, (a, b) in enumerate([
            (x_any, x_ref), (w_any, w_ref), (asrc_any, asrc_ref), (adst_any, adst_ref), (bias_any, bias_ref),
            (bits_any, bits)])
    ]
    for copy in loads:
        copy.start()
    for copy in loads[:4]:
        copy.wait()

    odd = (y + z) % 2
    block = jnp.where(odd == 0, y, z)
    index = jnp.where(odd == 0, z, y) // 2
    place = lax.broadcasted_iota(jnp.int32, (BLOCK, BLOCK), 0)
    node = lax.broadcasted_iota(jnp.int32, (BLOCK, BLOCK), 1)
    order = jnp.where(node == 8 * (place % 16) + place // 16, 1.0, 0.0).astype(BF16)
    feats[odd, block, index] = jnp.dot(order, x_ref[...], preferred_element_type=F32).astype(BF16)

    pl.semaphore_wait(barrier, 2 * (side - 1) + cols - 1)
    first = []
    for k in range(1, side):
        peer = at(jnp.where(odd == 0, y, (y + k) % side), jnp.where(odd == 0, (z + k) % side, z))
        mine = feats.at[odd, block, index]
        first.append(pltpu.make_async_remote_copy(
            mine, mine, one_send.at[k - 1], one_recv.at[k - 1], device_id=peer, device_id_type=MESH))
        first[-1].start()

    wt[...] = jnp.transpose(w_ref[...].astype(F32)).astype(BF16)
    rows[...] = attention_rows(asrc_ref[...], adst_ref[...])
    projected = project_t(wt[...], x_ref[...])
    own_score = scores_of(rows[...], projected)
    dme[...] = jnp.concatenate([own_score[HEADS:], own_score[:HEADS]], axis=0)
    scores = []
    for k in range(1, cols):
        scores.append(pltpu.make_async_remote_copy(
            dme, dall.at[c], d_send.at[k - 1], d_recv.at[k - 1],
            device_id=(r, (c + k) % cols), device_id_type=MESH))
        scores[-1].start()
    dall[c] = dme[...]
    raw = own_score[:HEADS] + own_score[HEADS:]
    self_weight = jnp.exp(leaky_relu(raw)).astype(BF16).astype(F32)
    own_weight[...] = jnp.concatenate([self_weight, jnp.zeros_like(self_weight)], axis=0)
    own_total[...] = jnp.concatenate(
        [projected[h * HEAD_DIM:(h + 1) * HEAD_DIM].astype(F32) * self_weight[h:h + 1] for h in range(HEADS)], axis=0)

    for copy in loads[4:]:
        copy.wait()

    def unpack(i, carry):
        d, slot = i // links, i % links
        live = jnp.where(slot < count_ref[0, d], 1, 0)
        words = (bits[d, slot] * live).astype(jnp.int16)
        for k in range(8):
            mask[d, slot, pl.ds(16 * k, 16)] = jnp.where(
                (words & (1 << k)) != 0, jnp.asarray(OPEN, BF16), jnp.asarray(0.0, BF16))
        return carry

    lax.fori_loop(0, bits.shape[0] * links, unpack, 0, unroll=4)

    for copy in first:
        copy.wait_recv()

    def second(half, way, stage):
        me = y if half == 0 else z
        hop = (1 if stage % 2 == 0 else 2) * (1 if way == 0 else -1)
        back = 0 if stage < 2 else (2 if way == 0 else -2)
        where = (me - back + side) % side
        if stage < 3:
            ref = feats.at[half, where]
        else:
            ref = feats.at[half, where, pl.ds(way * (quarter // 2), quarter // 2)]
        target = (me + hop + side) % side
        return pltpu.make_async_remote_copy(
            ref, ref, two_send.at[half, way, stage], two_recv.at[half, way, stage],
            device_id=at(target, z) if half == 0 else at(y, target), device_id_type=MESH)

    lanes = [(half, way) for half in range(2) for way in range(2)]
    sent = {(half, way, stage): second(half, way, stage) for stage in range(4) for half, way in lanes}
    for stage in (1, 0):
        for half, way in lanes:
            sent[half, way, stage].start()

    one_row = jnp.where(lax.broadcasted_iota(jnp.int32, (16, BLOCK), 0) == 0, 1.0, 0.0).astype(BF16)

    def prepare(half, where, largest):
        group = jnp.concatenate([feats[half, where, i] for i in range(quarter)], axis=0)
        values = project_t(wt[...], group)
        score = scores_of(rows[...], values)
        scale = jnp.exp(SLOPE * score).astype(BF16)
        rise = jnp.exp(RISE * score)
        for i in range(quarter):
            lane = slice(i * BLOCK, (i + 1) * BLOCK)
            across = 2 * i + (where + half) % 2
            source = jnp.where(half == 0, where * side + across, across * side + where)
            for h in range(HEADS):
                row = scale[h:h + 1, lane]
                vt[source, pl.ds(h * V_ROWS, HEAD_DIM)] = values[h * HEAD_DIM:(h + 1) * HEAD_DIM, lane] * row
                vt[source, pl.ds(h * V_ROWS + HEAD_DIM, 16)] = one_row * row
            column = jnp.transpose(rise[:, lane])
            for h in range(HEADS):
                eb[source, h] = jnp.broadcast_to(column[:, h:h + 1], (BLOCK, BLOCK)).astype(BF16)
        return jnp.maximum(largest, jnp.abs(score))

    def near(i, distance, largest):
        half, way = i // 2, i % 2
        me = jnp.where(half == 0, y, z)
        return prepare(half, (me + jnp.where(way == 0, -distance, distance) + side) % side, largest)

    largest = jnp.zeros((8, quarter * BLOCK), F32)
    largest = lax.fori_loop(0, 2, lambda i, m: near(2 * i, 0, m), largest)
    for half, way in lanes:
        sent[half, way, 1].wait_recv()
        sent[half, way, 2].start()
        sent[half, way, 3].start()
    for half, way in lanes:
        sent[half, way, 0].wait_recv()
    largest = lax.fori_loop(0, 8, lambda i, m: near(i % 4, 1 + i // 4, m), largest)
    for half, way in lanes:
        sent[half, way, 2].wait_recv()
    largest = lax.fori_loop(0, 4, lambda i, m: near(i, 3, m), largest)
    for half, way in lanes:
        sent[half, way, 3].wait_recv()
    largest = lax.fori_loop(0, 2, lambda i, m: near(2 * i, 4, m), largest)
    for copy in scores:
        copy.wait_recv()
    peak = jnp.broadcast_to(jnp.max(largest, axis=(0, 1), keepdims=True), (8, BLOCK))

    def send(k, d):
        return pltpu.make_async_remote_copy(
            parts.at[d], land.at[k - 1], rs_send.at[k - 1], rs_recv.at[k - 1], device_id=(r, d), device_id_type=MESH)

    def one_target(k, carry):
        d = (c + k) % cols
        target = dall[d]
        reach = jnp.exp(RISE * target).astype(BF16)
        fall = jnp.exp(SLOPE * target)
        sources = [src_ref[d, slot] for slot in range(links)]
        denominators = []
        for pair in range(HEADS // 2):
            weights = []
            for h in (2 * pair, 2 * pair + 1):
                mine = jnp.broadcast_to(reach[h:h + 1], (BLOCK, BLOCK))
                weights.append(jnp.concatenate([
                    jnp.minimum(jnp.maximum(eb[source, h] * mine, jnp.asarray(1.0, BF16)), mask[d, slot])
                    for slot, source in enumerate(sources)], axis=0))
            edge = jnp.concatenate(weights, axis=1)
            values = jnp.concatenate([vt[source, pl.ds(2 * pair * V_ROWS, 2 * V_ROWS)] for source in sources], axis=1)
            both = jnp.dot(values, edge, preferred_element_type=F32)
            for j in range(2):
                h = 2 * pair + j
                total = both[j * V_ROWS:(j + 1) * V_ROWS, j * BLOCK:(j + 1) * BLOCK] * fall[h:h + 1]
                parts[d, pl.ds(h * HEAD_DIM, HEAD_DIM)] = total[:HEAD_DIM].astype(BF16)
                denominators.append(total[HEAD_DIM:HEAD_DIM + 1])
        denominators += [jnp.zeros((8 - HEADS, BLOCK), F32), peak]
        parts[d, pl.ds(HID, 16)] = jnp.concatenate(denominators, axis=0).astype(BF16)

        @pl.when(k < cols)
        def _():
            send(k, d).start()

        return carry

    lax.fori_loop(1, cols + 1, one_target, 0)

    total = own_total[...] + parts[c, pl.ds(0, HID)].astype(F32)
    tail = parts[c, pl.ds(HID, 16)].astype(F32)
    denominator, peak = own_weight[...] + tail[:8], tail[8:]
    for k in range(1, cols):
        send(k, (c + k) % cols).wait_recv()
        total = total + land[k - 1, pl.ds(0, HID)].astype(F32)
        tail = land[k - 1, pl.ds(HID, 16)].astype(F32)
        denominator, peak = denominator + tail[:8], jnp.maximum(peak, tail[8:])
    blended = jnp.concatenate(
        [total[h * HEAD_DIM:(h + 1) * HEAD_DIM] / denominator[h:h + 1] for h in range(HEADS)], axis=0)
    value = jnp.transpose(blended) + bias_ref[...]
    out_ref[...] = jnp.where(value > 0, value, jnp.exp(jnp.minimum(value, 0.0)) - 1.0).astype(BF16)
    peak_ref[0, 0] = jnp.max(peak)
    for copy in first + scores + list(sent.values()):
        copy.wait_send()
    for k in range(1, cols):
        send(k, (c + k) % cols).wait_send()


def layer(side, cols, node_feats, weight, att_src, att_dst, out_bias, block_src, block_count, block_bits):
    vmem = pl.BlockSpec(memory_space=pltpu.VMEM)
    smem = pl.BlockSpec(memory_space=pltpu.SMEM)
    hbm = pl.BlockSpec(memory_space=pl.ANY)
    dma = pltpu.SemaphoreType.DMA
    sources = side * side
    dest, links = block_src.shape
    return pl.pallas_call(
        functools.partial(layer_kernel, side, cols),
        out_shape=(jax.ShapeDtypeStruct((BLOCK, HID), BF16), jax.ShapeDtypeStruct((1, 1), F32)),
        in_specs=[smem, smem] + [hbm] * 6,
        out_specs=(vmem, smem),
        scratch_shapes=[
            pltpu.VMEM((BLOCK, BLOCK), BF16),
            pltpu.VMEM((BLOCK, HID), BF16),
            pltpu.VMEM((1, HID), F32),
            pltpu.VMEM((1, HID), F32),
            pltpu.VMEM((1, HID), F32),
            pltpu.VMEM(block_bits.shape, jnp.int32),
            pltpu.VMEM((2, side, side // 2, BLOCK, BLOCK), BF16),
            pltpu.VMEM((8, BLOCK), F32),
            pltpu.VMEM((cols, 8, BLOCK), F32),
            pltpu.VMEM((HID, BLOCK), BF16),
            pltpu.VMEM((32, HID), BF16),
            pltpu.VMEM((sources, HEADS * V_ROWS, BLOCK), BF16),
            pltpu.VMEM((sources, HEADS, BLOCK, BLOCK), BF16),
            pltpu.VMEM((dest, links, BLOCK, BLOCK), BF16),
            pltpu.VMEM((cols, P_ROWS, BLOCK), BF16),
            pltpu.VMEM((cols - 1, P_ROWS, BLOCK), BF16),
            pltpu.VMEM((HID, BLOCK), F32),
            pltpu.VMEM((8, BLOCK), F32),
            dma((6,)), dma((cols - 1,)), dma((cols - 1,)), dma((side - 1,)), dma((side - 1,)),
            dma((2, 2, 4)), dma((2, 2, 4)), dma((cols - 1,)), dma((cols - 1,)),
        ],
        compiler_params=pltpu.CompilerParams(
            collective_id=0, has_side_effects=True, vmem_limit_bytes=56 * 1024 * 1024),
        name="attention_layer",
    )(block_src, block_count, node_feats, weight, att_src, att_dst, out_bias, block_bits)


def vector_rows(att):
    high = att.astype(BF16).astype(F32)
    middle = (att - high).astype(BF16).astype(F32)
    low = att - high - middle
    row = lax.broadcasted_iota(jnp.int32, (32, HID), 0)
    column = lax.broadcasted_iota(jnp.int32, (32, HID), 1)
    piece = jnp.where(row < 8, high, jnp.where(row < 16, middle, low))
    return jnp.where((row % 8 == column // HEAD_DIM) & (row < 24), piece, 0.0).astype(BF16)


def transposed(weight):
    return jnp.transpose(weight.astype(F32)).astype(BF16)


def gather_kernel(side, cols, x_ref, w_ref, adst_ref, ga_ref, gb_ref, d_ref, xp, dme,
                  local_sem, d_send, d_recv, one_send, one_recv, two_send, two_recv):
    r, c = lax.axis_index("rows"), lax.axis_index("cols")
    y, z = r // side, r % side

    def at(yy, zz):
        return (yy * side + zz, c)

    barrier = pltpu.get_barrier_semaphore()
    for k in range(1, side):
        pl.semaphore_signal(barrier, inc=1, device_id=at(y, (z + k) % side), device_id_type=MESH)
        pl.semaphore_signal(barrier, inc=1, device_id=at((y + k) % side, z), device_id_type=MESH)
    for k in range(1, cols):
        pl.semaphore_signal(barrier, inc=1, device_id=(r, (c + k) % cols), device_id_type=MESH)

    place = lax.broadcasted_iota(jnp.int32, (BLOCK, BLOCK), 0)
    node = lax.broadcasted_iota(jnp.int32, (BLOCK, BLOCK), 1)
    order = jnp.where(node == 8 * (place % 16) + place // 16, 1.0, 0.0).astype(BF16)
    xp[...] = jnp.dot(order, x_ref[...], preferred_element_type=F32).astype(BF16)
    dme[...] = scores_of(vector_rows(adst_ref[...]), project_t(transposed(w_ref[...]), x_ref[...]))
    pl.semaphore_wait(barrier, 2 * (side - 1) + cols - 1)

    first = []
    for k in range(1, side):
        first.append(pltpu.make_async_remote_copy(
            xp.at[pl.ds(0, HALF)], ga_ref.at[y, z], one_send.at[0, k - 1], one_recv.at[0, k - 1],
            device_id=at(y, (z + k) % side), device_id_type=MESH))
        first.append(pltpu.make_async_remote_copy(
            xp.at[pl.ds(HALF, HALF)], gb_ref.at[z, y], one_send.at[1, k - 1], one_recv.at[1, k - 1],
            device_id=at((y + k) % side, z), device_id_type=MESH))
    for copy in first:
        copy.start()
    own = [
        pltpu.make_async_copy(xp.at[pl.ds(0, HALF)], ga_ref.at[y, z], local_sem.at[0]),
        pltpu.make_async_copy(xp.at[pl.ds(HALF, HALF)], gb_ref.at[z, y], local_sem.at[1]),
        pltpu.make_async_copy(dme, d_ref.at[c], local_sem.at[2]),
    ]
    for copy in own:
        copy.start()
    scores = []
    for k in range(1, cols):
        scores.append(pltpu.make_async_remote_copy(
            dme, d_ref.at[c], d_send.at[k - 1], d_recv.at[k - 1],
            device_id=(r, (c + k) % cols), device_id_type=MESH))
        scores[-1].start()
    for copy in own:
        copy.wait()
    for copy in first:
        copy.wait_recv()

    sub = side // 2
    half_way = side // 2

    def second(half, way, step, part):
        buffer, place = (ga_ref, y) if half == 0 else (gb_ref, z)
        if way == 0:
            block, target = (place - step + 1 + side) % side, (place + 1) % side
        else:
            block, target = (place + step - 1) % side, (place + side - 1) % side
        ref = buffer.at[block, pl.ds(part * sub, sub)]
        return pltpu.make_async_remote_copy(
            ref, ref, two_send.at[half, way, step - 1, part], two_recv.at[half, way, step - 1, part],
            device_id=at(target, z) if half == 0 else at(y, target), device_id_type=MESH)

    lanes = [(half, way) for half in range(2) for way in range(2)]
    inflight = {}
    for step in range(1, half_way + 1):
        for part in range(2):
            for half, way in lanes:
                if step > 1:
                    inflight[half, way, step - 1, part].wait_recv()
                if step < half_way or part == way:
                    inflight[half, way, step, part] = second(half, way, step, part)
                    inflight[half, way, step, part].start()
    for half, way in lanes:
        inflight[half, way, half_way, way].wait_recv()
    for copy in scores:
        copy.wait_recv()
    for copy in first + scores + list(inflight.values()):
        copy.wait_send()


def gather(side, cols, node_feats, weight, att_dst):
    vmem = pl.BlockSpec(memory_space=pltpu.VMEM)
    hbm = pl.BlockSpec(memory_space=pl.ANY)
    dma = pltpu.SemaphoreType.DMA
    return pl.pallas_call(
        functools.partial(gather_kernel, side, cols),
        out_shape=(
            jax.ShapeDtypeStruct((side, side, HALF, BLOCK), BF16),
            jax.ShapeDtypeStruct((side, side, HALF, BLOCK), BF16),
            jax.ShapeDtypeStruct((cols, 8, BLOCK), F32),
        ),
        in_specs=[vmem, vmem, vmem],
        out_specs=(hbm, hbm, hbm),
        scratch_shapes=[
            pltpu.VMEM((BLOCK, BLOCK), BF16),
            pltpu.VMEM((8, BLOCK), F32),
            dma((3,)), dma((cols - 1,)), dma((cols - 1,)),
            dma((2, side - 1)), dma((2, side - 1)),
            dma((2, 2, side // 2, 2)), dma((2, 2, side // 2, 2)),
        ],
        compiler_params=pltpu.CompilerParams(collective_id=1, has_side_effects=True),
        name="gather_features",
    )(node_feats, weight, att_dst)


def aggregate_kernel(side, src_ref, count_ref, bits_ref, ga_ref, gb_ref, d_ref, w_ref, asrc_ref, p_ref,
                     vt, st, acc):
    dest = d_ref.shape[0]
    weight_t = transposed(w_ref[...])
    rows = vector_rows(asrc_ref[...])
    ones_row = jnp.where(lax.broadcasted_iota(jnp.int32, (16, BLOCK), 0) == 0, 1.0, 0.0)

    def blocks_of(y):
        pieces = []
        for z in range(side):
            pieces += [ga_ref[y, z], gb_ref[z, y]]
        feats = jnp.concatenate(pieces, axis=0)
        projected = project_t(weight_t, feats)
        return projected, scores_of(rows, projected)

    def run(weights_of, finish):
        def one_row(d, carry):
            acc[...] = jnp.zeros_like(acc)
            own = d_ref[d]

            def one_group(g, inner):
                slots = [g * GROUP + i for i in range(GROUP)]
                blocks = [src_ref[d, slot] for slot in slots]
                per_slot = [weights_of(d, slot, block, own) for slot, block in zip(slots, blocks)]
                for h in range(HEADS):
                    edge = jnp.concatenate([piece for one in per_slot for piece in one[h]], axis=0)
                    values = jnp.concatenate([vt[block, h] for block in blocks], axis=1)
                    acc[h] += jnp.dot(values, edge, preferred_element_type=F32)
                return inner

            lax.fori_loop(0, count_ref[d] // GROUP, one_group, 0)
            finish(d, own)
            return carry

        lax.fori_loop(0, dest, one_row, 0)

    def store(d, factor):
        denominators = []
        for h in range(HEADS):
            scaled = acc[h] * factor[h:h + 1, :]
            p_ref[d, pl.ds(h * HEAD_DIM, HEAD_DIM)] = scaled[:HEAD_DIM].astype(BF16)
            denominators.append(scaled[HEAD_DIM:HEAD_DIM + 1])
        denominators.append(jnp.zeros((16 - HEADS, BLOCK), F32))
        p_ref[d, pl.ds(HID, 16)] = jnp.concatenate(denominators, axis=0).astype(BF16)

    def direct(d, slot, block, own):
        words = bits_ref[d, slot]
        live = jnp.concatenate([jnp.right_shift(words, k) & 1 for k in range(8)], axis=0) != 0
        result = []
        for h in range(HEADS):
            raw = st[block, :, pl.ds(h, 1)] + own[h:h + 1, :]
            result.append([jnp.where(live, jnp.exp(leaky_relu(raw)), 0.0).astype(BF16)])
        return result

    def prepare_direct(y, carry):
        projected, score = blocks_of(y)
        for z in range(side):
            at = slice(z * BLOCK, (z + 1) * BLOCK)
            block = y * side + z
            for h in range(HEADS):
                values = projected[h * HEAD_DIM:(h + 1) * HEAD_DIM, at].astype(F32)
                vt[block, h] = jnp.concatenate([values, ones_row], axis=0).astype(BF16)
            st[block] = jnp.transpose(score[:, at])
        return carry

    lax.fori_loop(0, side, prepare_direct, 0)
    run(direct, lambda d, own: store(d, jnp.ones_like(own)))


def aggregate(side, block_src, block_count, block_bits, ga, gb, target_scores, weight, att_src):
    vmem = pl.BlockSpec(memory_space=pltpu.VMEM)
    smem = pl.BlockSpec(memory_space=pltpu.SMEM)
    dest = block_src.shape[0]
    sources = side * side
    return pl.pallas_call(
        functools.partial(aggregate_kernel, side),
        out_shape=jax.ShapeDtypeStruct((dest, SUM_ROWS, BLOCK), BF16),
        in_specs=[smem, smem, vmem, vmem, vmem, vmem, vmem, vmem],
        out_specs=vmem,
        scratch_shapes=[
            pltpu.VMEM((sources, HEADS, V_ROWS, BLOCK), BF16),
            pltpu.VMEM((sources, BLOCK, 8), F32),
            pltpu.VMEM((HEADS, V_ROWS, BLOCK), F32),
        ],
        compiler_params=pltpu.CompilerParams(vmem_limit_bytes=40 * 1024 * 1024),
        name="aggregate_edges",
    )(block_src, block_count, block_bits, ga, gb, target_scores, weight, att_src)


def combine_kernel(cols, p_ref, x_ref, w_ref, asrc_ref, adst_ref, bias_ref, out_ref, land, send, recv):
    r, c = lax.axis_index("rows"), lax.axis_index("cols")
    barrier = pltpu.get_barrier_semaphore()
    for k in range(1, cols):
        pl.semaphore_signal(barrier, inc=1, device_id=(r, (c + k) % cols), device_id_type=MESH)
    pl.semaphore_wait(barrier, cols - 1)
    copies = []
    for k in range(1, cols):
        peer = (c + k) % cols
        copies.append(pltpu.make_async_remote_copy(
            p_ref.at[peer], land.at[k - 1], send.at[k - 1], recv.at[k - 1],
            device_id=(r, peer), device_id_type=MESH))
        copies[-1].start()

    projected = project_t(transposed(w_ref[...]), x_ref[...])
    raw = scores_of(vector_rows(asrc_ref[...]), projected) + scores_of(vector_rows(adst_ref[...]), projected)
    self_weight = jnp.exp(leaky_relu(raw)).astype(BF16).astype(F32)
    own = p_ref[c].astype(F32)
    numerator = [
        own[h * HEAD_DIM:(h + 1) * HEAD_DIM]
        + projected[h * HEAD_DIM:(h + 1) * HEAD_DIM].astype(F32) * self_weight[h:h + 1]
        for h in range(HEADS)
    ]
    total = jnp.concatenate(numerator, axis=0)
    denominator = own[HID:HID + 8] + self_weight
    for k, copy in enumerate(copies):
        copy.wait_recv()
        total = total + land[k, pl.ds(0, HID)].astype(F32)
        denominator = denominator + land[k, pl.ds(HID, 16)].astype(F32)[:8]
    blended = jnp.concatenate(
        [total[h * HEAD_DIM:(h + 1) * HEAD_DIM] / denominator[h:h + 1] for h in range(HEADS)], axis=0)
    value = jnp.transpose(blended) + bias_ref[...]
    out_ref[...] = jnp.where(value > 0, value, jnp.exp(jnp.minimum(value, 0.0)) - 1.0).astype(BF16)
    for copy in copies:
        copy.wait_send()


def combine(cols, partials, node_feats, weight, att_src, att_dst, out_bias):
    vmem = pl.BlockSpec(memory_space=pltpu.VMEM)
    return pl.pallas_call(
        functools.partial(combine_kernel, cols),
        out_shape=jax.ShapeDtypeStruct((BLOCK, HID), BF16),
        in_specs=[vmem] * 6,
        out_specs=vmem,
        scratch_shapes=[
            pltpu.VMEM((cols - 1, SUM_ROWS, BLOCK), BF16),
            pltpu.SemaphoreType.DMA((cols - 1,)),
            pltpu.SemaphoreType.DMA((cols - 1,)),
        ],
        compiler_params=pltpu.CompilerParams(collective_id=2, has_side_effects=True),
        name="combine_partials",
    )(partials, node_feats, weight, att_src, att_dst, out_bias)


def direct_shards(side, cols, node_feats, weight, att_src, att_dst, out_bias, block_src, block_count, block_bits):
    att_src, att_dst, out_bias = (v.reshape(1, HID) for v in (att_src, att_dst, out_bias))
    ga, gb, target_scores = gather(side, cols, node_feats, weight, att_dst)
    partials = aggregate(
        side, block_src[0], block_count[0], block_bits[0], ga, gb, target_scores, weight, att_src)
    return combine(cols, partials, node_feats, weight, att_src, att_dst, out_bias)


def shards(side, cols, *args):
    node_feats, weight, att_src, att_dst, out_bias, block_src, block_count, block_bits = args
    result, peak = layer(
        side, cols, node_feats, weight, att_src.reshape(1, HID), att_dst.reshape(1, HID), out_bias.reshape(1, HID),
        block_src[0], block_count, block_bits[0])
    return lax.cond(peak[0, 0] <= SAFE, lambda *rest: result, functools.partial(direct_shards, side, cols), *args)


def solution(mesh):
    side = math.isqrt(mesh.shape["rows"])
    cols = mesh.shape["cols"]
    in_specs = (
        P(("rows", "cols"), None),
        P(),
        P(),
        P(),
        P(),
        P(("rows", "cols"), None, None),
        P(("rows", "cols"), None),
        P(("rows", "cols"), None, None, None, None),
    )
    return jax.shard_map(
        functools.partial(shards, side, cols), mesh=mesh, in_specs=in_specs,
        out_specs=P(("rows", "cols"), None), check_vma=False)
```

```python
import functools
import math

import jax
import jax.numpy as jnp
from jax import lax
from jax.experimental import pallas as pl
from jax.experimental.pallas import tpu as pltpu
from jax.sharding import PartitionSpec as P

HEADS = 4
BLOCK = 128
HEAD_DIM = 64
HID = HEADS * HEAD_DIM
SLOPE = 0.2
RISE = 1.0 - SLOPE
SAFE = 100.0
V_ROWS = 80
P_ROWS = HID + 16
OPEN = float(jnp.finfo(jnp.bfloat16).max)
HALF = BLOCK // 2
SUM_ROWS = HID + 16
GROUP = 4
MESH = pl.DeviceIdType.MESH
F32 = jnp.float32
BF16 = jnp.bfloat16
NT = (((1,), (1,)), ((), ()))


def leaky_relu(raw_score):
    return jnp.where(raw_score > 0, raw_score, SLOPE * raw_score)


def attention_rows(att_src, att_dst):
    row = lax.broadcasted_iota(jnp.int32, (32, HID), 0)
    column = lax.broadcasted_iota(jnp.int32, (32, HID), 1)
    att = jnp.where(row % 8 < HEADS, att_src, att_dst)
    high = att.astype(BF16).astype(F32)
    middle = (att - high).astype(BF16).astype(F32)
    low = att - high - middle
    piece = jnp.where(row < 8, high, jnp.where(row < 16, middle, low))
    return jnp.where((row % HEADS == column // HEAD_DIM) & (row < 24), piece, 0.0).astype(BF16)


def scores_of(rows, projected_t):
    parts = jnp.dot(rows, projected_t, preferred_element_type=F32)
    return parts[0:8] + parts[8:16] + parts[16:24]


def project_t(weight_t, feats):
    return lax.dot_general(weight_t, feats, NT, preferred_element_type=F32).astype(BF16)


def layer_kernel(side, cols, src_ref, count_ref, x_any, w_any, asrc_any, adst_any, bias_any, bits_any, out_ref, peak_ref,
                 x_ref, w_ref, asrc_ref, adst_ref, bias_ref, bits, feats, dme, dall, wt, rows, vt, eb, mask, parts, land,
                 own_total, own_weight, load_sem, d_send, d_recv, one_send, one_recv, two_send, two_recv, rs_send, rs_recv):
    r, c = lax.axis_index("rows"), lax.axis_index("cols")
    y, z = r // side, r % side
    quarter = side // 2
    links = bits.shape[1]

    def at(yy, zz):
        return (yy * side + zz, c)

    loads = [
        pltpu.make_async_copy(a, b, load_sem.at[i])
        for i, (a, b) in enumerate([
            (x_any, x_ref), (w_any, w_ref), (asrc_any, asrc_ref), (adst_any, adst_ref), (bias_any, bias_ref),
            (bits_any, bits)])
    ]
    for copy in loads:
        copy.start()

    barrier = pltpu.get_barrier_semaphore()
    for k in range(1, side):
        pl.semaphore_signal(barrier, inc=1, device_id=at(y, (z + k) % side), device_id_type=MESH)
        pl.semaphore_signal(barrier, inc=1, device_id=at((y + k) % side, z), device_id_type=MESH)
    for k in range(1, cols):
        pl.semaphore_signal(barrier, inc=1, device_id=(r, (c + k) % cols), device_id_type=MESH)

    for copy in loads[:4]:
        copy.wait()

    odd = (y + z) % 2
    block = jnp.where(odd == 0, y, z)
    index = jnp.where(odd == 0, z, y) // 2
    place = lax.broadcasted_iota(jnp.int32, (BLOCK, BLOCK), 0)
    node = lax.broadcasted_iota(jnp.int32, (BLOCK, BLOCK), 1)
    order = jnp.where(node == 8 * (place % 16) + place // 16, 1.0, 0.0).astype(BF16)
    feats[odd, block, index] = jnp.dot(order, x_ref[...], preferred_element_type=F32).astype(BF16)

    pl.semaphore_wait(barrier, 2 * (side - 1) + cols - 1)
    first = []
    for k in range(1, side):
        peer = at(jnp.where(odd == 0, y, (y + k) % side), jnp.where(odd == 0, (z + k) % side, z))
        mine = feats.at[odd, block, index]
        first.append(pltpu.make_async_remote_copy(
            mine, mine, one_send.at[k - 1], one_recv.at[k - 1], device_id=peer, device_id_type=MESH))
        first[-1].start()

    halves = (odd, 1 - odd)
    sent = {}

    def along(half, delta):
        target_y = jnp.where(half == 0, (y + delta + side) % side, y)
        target_z = jnp.where(half == 0, z, (z + delta + side) % side)
        return at(target_y, target_z)

    def pass_on(role, way, step, piece):
        half = halves[role]
        me, across = jnp.where(half == 0, y, z), jnp.where(half == 0, z, y)
        sign = 1 if way == 0 else -1
        origin = (me - sign * (step - 1) + side) % side
        same = (role + step - 1) % 2 == 0
        offset = ((0, 2, -2, 4) if same else (1, -1, 3, -3))[piece]
        ref = feats.at[half, origin, (across + offset + side) % side // 2]
        copy = pltpu.make_async_remote_copy(
            ref, ref, two_send.at[half, way, step - 1, piece], two_recv.at[half, way, step - 1, piece],
            device_id=along(half, sign), device_id_type=MESH)
        copy.start()
        sent[role, way, step, piece] = copy

    lanes = [(role, way) for role in range(2) for way in range(2)]

    def forward(step, pieces):
        for piece in pieces:
            for role, way in lanes:
                arrive(role, way, step - 1, piece)
                if step < side // 2 or piece // 2 == way:
                    pass_on(role, way, step, piece)

    def arrive(role, way, step, piece):
        sent[role, way, step, piece].wait_recv()

    for way in range(2):
        pass_on(0, way, 1, 0)

    wt[...] = jnp.transpose(w_ref[...].astype(F32)).astype(BF16)
    rows[...] = attention_rows(asrc_ref[...], adst_ref[...])
    projected = project_t(wt[...], x_ref[...])
    own_score = scores_of(rows[...], projected)
    dme[...] = jnp.concatenate([own_score[HEADS:], own_score[:HEADS]], axis=0)
    scores = []
    for k in range(1, cols):
        scores.append(pltpu.make_async_remote_copy(
            dme, dall.at[c], d_send.at[k - 1], d_recv.at[k - 1],
            device_id=(r, (c + k) % cols), device_id_type=MESH))
        scores[-1].start()
    dall[c] = dme[...]
    raw = own_score[:HEADS] + own_score[HEADS:]
    self_weight = jnp.exp(leaky_relu(raw)).astype(BF16).astype(F32)
    own_weight[...] = jnp.concatenate([self_weight, jnp.zeros_like(self_weight)], axis=0)
    own_total[...] = jnp.concatenate(
        [projected[h * HEAD_DIM:(h + 1) * HEAD_DIM].astype(F32) * self_weight[h:h + 1] for h in range(HEADS)], axis=0)

    for copy in loads[4:]:
        copy.wait()

    def unpack(i, carry):
        d, slot = i // links, i % links
        live = jnp.where(slot < count_ref[0, d], 1, 0)
        words = (bits[d, slot] * live).astype(jnp.int16)
        for k in range(8):
            mask[d, slot, pl.ds(16 * k, 16)] = jnp.where(
                (words & (1 << k)) != 0, jnp.asarray(OPEN, BF16), jnp.asarray(0.0, BF16))
        return carry

    lax.fori_loop(0, bits.shape[0] * links, unpack, 0, unroll=4)

    for role, piece, distance in ((1, 0, 7), (1, 1, 1), (0, 1, 6), (0, 2, 2), (1, 2, 5), (1, 3, 3), (0, 3, 4)):
        first[distance - 1].wait_recv()
        for way in range(2):
            pass_on(role, way, 1, piece)

    one_row = jnp.where(lax.broadcasted_iota(jnp.int32, (16, BLOCK), 0) == 0, 1.0, 0.0).astype(BF16)

    def prepare(half, where, largest):
        group = jnp.concatenate([feats[half, where, i] for i in range(quarter)], axis=0)
        values = project_t(wt[...], group)
        score = scores_of(rows[...], values)
        scale = jnp.exp(SLOPE * score).astype(BF16)
        rise = jnp.exp(RISE * score)
        for i in range(quarter):
            lane = slice(i * BLOCK, (i + 1) * BLOCK)
            across = 2 * i + (where + half) % 2
            source = jnp.where(half == 0, where * side + across, across * side + where)
            for h in range(HEADS):
                row = scale[h:h + 1, lane]
                vt[source, pl.ds(h * V_ROWS, HEAD_DIM)] = values[h * HEAD_DIM:(h + 1) * HEAD_DIM, lane] * row
                vt[source, pl.ds(h * V_ROWS + HEAD_DIM, 16)] = one_row * row
            column = jnp.transpose(rise[:, lane]).astype(BF16)
            for h in range(HEADS):
                eb[source, h] = jnp.broadcast_to(column[:, h:h + 1], (BLOCK, BLOCK))
        return jnp.maximum(largest, jnp.abs(score))

    def near(half, distance, largest):
        me = jnp.where(half == 0, y, z)
        largest = prepare(half, (me - distance + side) % side, largest)
        return prepare(half, (me + distance) % side, largest)

    largest = jnp.zeros((8, quarter * BLOCK), F32)
    forward(2, (0, 1))
    largest = prepare(0, y, largest)
    forward(2, (2,))
    largest = prepare(1, z, largest)
    forward(2, (3,))
    for step in (3, 4):
        distance = step - 2
        largest = prepare(0, (y - distance + side) % side, largest)
        forward(step, (0,))
        largest = prepare(0, (y + distance) % side, largest)
        forward(step, (1,))
        largest = prepare(1, (z - distance + side) % side, largest)
        forward(step, (2,))
        largest = prepare(1, (z + distance) % side, largest)
        forward(step, (3,))
    largest = lax.fori_loop(0, 2, lambda half, m: near(half, 3, m), largest)
    for role, way in lanes:
        for piece in (2 * way, 2 * way + 1):
            arrive(role, way, side // 2, piece)
    largest = prepare(0, (y + side // 2) % side, largest)
    largest = prepare(1, (z + side // 2) % side, largest)
    for copy in scores:
        copy.wait_recv()
    peak = jnp.broadcast_to(jnp.max(largest, axis=(0, 1), keepdims=True), (8, BLOCK))

    def send(k, d):
        return pltpu.make_async_remote_copy(
            parts.at[d], land.at[k - 1], rs_send.at[k - 1], rs_recv.at[k - 1], device_id=(r, d), device_id_type=MESH)

    def one_target(k, carry):
        d = (c + k) % cols
        target = dall[d]
        reach = jnp.exp(RISE * target).astype(BF16)
        fall = jnp.exp(SLOPE * target)
        sources = [src_ref[d, slot] for slot in range(links)]
        denominators = []
        for pair in range(HEADS // 2):
            weights = []
            for h in (2 * pair, 2 * pair + 1):
                mine = jnp.broadcast_to(reach[h:h + 1], (BLOCK, BLOCK))
                weights.append(jnp.concatenate([
                    jnp.minimum(jnp.maximum(eb[source, h] * mine, jnp.asarray(1.0, BF16)), mask[d, slot])
                    for slot, source in enumerate(sources)], axis=0))
            edge = jnp.concatenate(weights, axis=1)
            values = jnp.concatenate([vt[source, pl.ds(2 * pair * V_ROWS, 2 * V_ROWS)] for source in sources], axis=1)
            both = jnp.dot(values, edge, preferred_element_type=F32)
            for j in range(2):
                h = 2 * pair + j
                total = both[j * V_ROWS:(j + 1) * V_ROWS, j * BLOCK:(j + 1) * BLOCK] * fall[h:h + 1]
                parts[d, pl.ds(h * HEAD_DIM, HEAD_DIM)] = total[:HEAD_DIM].astype(BF16)
                denominators.append(total[HEAD_DIM:HEAD_DIM + 1])
        denominators += [jnp.zeros((8 - HEADS, BLOCK), F32), peak]
        parts[d, pl.ds(HID, 16)] = jnp.concatenate(denominators, axis=0).astype(BF16)

        @pl.when(k < cols)
        def _():
            send(k, d).start()

        return carry

    lax.fori_loop(1, cols + 1, one_target, 0)

    total = own_total[...] + parts[c, pl.ds(0, HID)].astype(F32)
    tail = parts[c, pl.ds(HID, 16)].astype(F32)
    denominator, peak = own_weight[...] + tail[:8], tail[8:]
    for k in range(1, cols):
        send(k, (c + k) % cols).wait_recv()
        total = total + land[k - 1, pl.ds(0, HID)].astype(F32)
        tail = land[k - 1, pl.ds(HID, 16)].astype(F32)
        denominator, peak = denominator + tail[:8], jnp.maximum(peak, tail[8:])
    blended = jnp.concatenate(
        [total[h * HEAD_DIM:(h + 1) * HEAD_DIM] / denominator[h:h + 1] for h in range(HEADS)], axis=0)
    value = jnp.transpose(blended) + bias_ref[...]
    out_ref[...] = jnp.where(value > 0, value, jnp.exp(jnp.minimum(value, 0.0)) - 1.0).astype(BF16)
    peak_ref[0, 0] = jnp.max(peak)
    for copy in first + scores + list(sent.values()):
        copy.wait_send()
    for k in range(1, cols):
        send(k, (c + k) % cols).wait_send()


def layer(side, cols, node_feats, weight, att_src, att_dst, out_bias, block_src, block_count, block_bits):
    vmem = pl.BlockSpec(memory_space=pltpu.VMEM)
    smem = pl.BlockSpec(memory_space=pltpu.SMEM)
    hbm = pl.BlockSpec(memory_space=pl.ANY)
    dma = pltpu.SemaphoreType.DMA
    sources = side * side
    dest, links = block_src.shape
    return pl.pallas_call(
        functools.partial(layer_kernel, side, cols),
        out_shape=(jax.ShapeDtypeStruct((BLOCK, HID), BF16), jax.ShapeDtypeStruct((1, 1), F32)),
        in_specs=[smem, smem] + [hbm] * 6,
        out_specs=(vmem, smem),
        scratch_shapes=[
            pltpu.VMEM((BLOCK, BLOCK), BF16),
            pltpu.VMEM((BLOCK, HID), BF16),
            pltpu.VMEM((1, HID), F32),
            pltpu.VMEM((1, HID), F32),
            pltpu.VMEM((1, HID), F32),
            pltpu.VMEM(block_bits.shape, jnp.int32),
            pltpu.VMEM((2, side, side // 2, BLOCK, BLOCK), BF16),
            pltpu.VMEM((8, BLOCK), F32),
            pltpu.VMEM((cols, 8, BLOCK), F32),
            pltpu.VMEM((HID, BLOCK), BF16),
            pltpu.VMEM((32, HID), BF16),
            pltpu.VMEM((sources, HEADS * V_ROWS, BLOCK), BF16),
            pltpu.VMEM((sources, HEADS, BLOCK, BLOCK), BF16),
            pltpu.VMEM((dest, links, BLOCK, BLOCK), BF16),
            pltpu.VMEM((cols, P_ROWS, BLOCK), BF16),
            pltpu.VMEM((cols - 1, P_ROWS, BLOCK), BF16),
            pltpu.VMEM((HID, BLOCK), F32),
            pltpu.VMEM((8, BLOCK), F32),
            dma((6,)), dma((cols - 1,)), dma((cols - 1,)), dma((side - 1,)), dma((side - 1,)),
            dma((2, 2, side // 2, side // 2)), dma((2, 2, side // 2, side // 2)), dma((cols - 1,)), dma((cols - 1,)),
        ],
        compiler_params=pltpu.CompilerParams(
            collective_id=0, has_side_effects=True, vmem_limit_bytes=56 * 1024 * 1024),
        name="attention_layer",
    )(block_src, block_count, node_feats, weight, att_src, att_dst, out_bias, block_bits)


def vector_rows(att):
    high = att.astype(BF16).astype(F32)
    middle = (att - high).astype(BF16).astype(F32)
    low = att - high - middle
    row = lax.broadcasted_iota(jnp.int32, (32, HID), 0)
    column = lax.broadcasted_iota(jnp.int32, (32, HID), 1)
    piece = jnp.where(row < 8, high, jnp.where(row < 16, middle, low))
    return jnp.where((row % 8 == column // HEAD_DIM) & (row < 24), piece, 0.0).astype(BF16)


def transposed(weight):
    return jnp.transpose(weight.astype(F32)).astype(BF16)


def gather_kernel(side, cols, x_ref, w_ref, adst_ref, ga_ref, gb_ref, d_ref, xp, dme,
                  local_sem, d_send, d_recv, one_send, one_recv, two_send, two_recv):
    r, c = lax.axis_index("rows"), lax.axis_index("cols")
    y, z = r // side, r % side

    def at(yy, zz):
        return (yy * side + zz, c)

    barrier = pltpu.get_barrier_semaphore()
    for k in range(1, side):
        pl.semaphore_signal(barrier, inc=1, device_id=at(y, (z + k) % side), device_id_type=MESH)
        pl.semaphore_signal(barrier, inc=1, device_id=at((y + k) % side, z), device_id_type=MESH)
    for k in range(1, cols):
        pl.semaphore_signal(barrier, inc=1, device_id=(r, (c + k) % cols), device_id_type=MESH)

    place = lax.broadcasted_iota(jnp.int32, (BLOCK, BLOCK), 0)
    node = lax.broadcasted_iota(jnp.int32, (BLOCK, BLOCK), 1)
    order = jnp.where(node == 8 * (place % 16) + place // 16, 1.0, 0.0).astype(BF16)
    xp[...] = jnp.dot(order, x_ref[...], preferred_element_type=F32).astype(BF16)
    dme[...] = scores_of(vector_rows(adst_ref[...]), project_t(transposed(w_ref[...]), x_ref[...]))
    pl.semaphore_wait(barrier, 2 * (side - 1) + cols - 1)

    first = []
    for k in range(1, side):
        first.append(pltpu.make_async_remote_copy(
            xp.at[pl.ds(0, HALF)], ga_ref.at[y, z], one_send.at[0, k - 1], one_recv.at[0, k - 1],
            device_id=at(y, (z + k) % side), device_id_type=MESH))
        first.append(pltpu.make_async_remote_copy(
            xp.at[pl.ds(HALF, HALF)], gb_ref.at[z, y], one_send.at[1, k - 1], one_recv.at[1, k - 1],
            device_id=at((y + k) % side, z), device_id_type=MESH))
    for copy in first:
        copy.start()
    own = [
        pltpu.make_async_copy(xp.at[pl.ds(0, HALF)], ga_ref.at[y, z], local_sem.at[0]),
        pltpu.make_async_copy(xp.at[pl.ds(HALF, HALF)], gb_ref.at[z, y], local_sem.at[1]),
        pltpu.make_async_copy(dme, d_ref.at[c], local_sem.at[2]),
    ]
    for copy in own:
        copy.start()
    scores = []
    for k in range(1, cols):
        scores.append(pltpu.make_async_remote_copy(
            dme, d_ref.at[c], d_send.at[k - 1], d_recv.at[k - 1],
            device_id=(r, (c + k) % cols), device_id_type=MESH))
        scores[-1].start()
    for copy in own:
        copy.wait()
    for copy in first:
        copy.wait_recv()

    sub = side // 2
    half_way = side // 2

    def second(half, way, step, part):
        buffer, place = (ga_ref, y) if half == 0 else (gb_ref, z)
        if way == 0:
            block, target = (place - step + 1 + side) % side, (place + 1) % side
        else:
            block, target = (place + step - 1) % side, (place + side - 1) % side
        ref = buffer.at[block, pl.ds(part * sub, sub)]
        return pltpu.make_async_remote_copy(
            ref, ref, two_send.at[half, way, step - 1, part], two_recv.at[half, way, step - 1, part],
            device_id=at(target, z) if half == 0 else at(y, target), device_id_type=MESH)

    lanes = [(half, way) for half in range(2) for way in range(2)]
    inflight = {}
    for step in range(1, half_way + 1):
        for part in range(2):
            for half, way in lanes:
                if step > 1:
                    inflight[half, way, step - 1, part].wait_recv()
                if step < half_way or part == way:
                    inflight[half, way, step, part] = second(half, way, step, part)
                    inflight[half, way, step, part].start()
    for half, way in lanes:
        inflight[half, way, half_way, way].wait_recv()
    for copy in scores:
        copy.wait_recv()
    for copy in first + scores + list(inflight.values()):
        copy.wait_send()


def gather(side, cols, node_feats, weight, att_dst):
    vmem = pl.BlockSpec(memory_space=pltpu.VMEM)
    hbm = pl.BlockSpec(memory_space=pl.ANY)
    dma = pltpu.SemaphoreType.DMA
    return pl.pallas_call(
        functools.partial(gather_kernel, side, cols),
        out_shape=(
            jax.ShapeDtypeStruct((side, side, HALF, BLOCK), BF16),
            jax.ShapeDtypeStruct((side, side, HALF, BLOCK), BF16),
            jax.ShapeDtypeStruct((cols, 8, BLOCK), F32),
        ),
        in_specs=[vmem, vmem, vmem],
        out_specs=(hbm, hbm, hbm),
        scratch_shapes=[
            pltpu.VMEM((BLOCK, BLOCK), BF16),
            pltpu.VMEM((8, BLOCK), F32),
            dma((3,)), dma((cols - 1,)), dma((cols - 1,)),
            dma((2, side - 1)), dma((2, side - 1)),
            dma((2, 2, side // 2, 2)), dma((2, 2, side // 2, 2)),
        ],
        compiler_params=pltpu.CompilerParams(collective_id=1, has_side_effects=True),
        name="gather_features",
    )(node_feats, weight, att_dst)


def aggregate_kernel(side, src_ref, count_ref, bits_ref, ga_ref, gb_ref, d_ref, w_ref, asrc_ref, p_ref,
                     vt, st, acc):
    dest = d_ref.shape[0]
    weight_t = transposed(w_ref[...])
    rows = vector_rows(asrc_ref[...])
    ones_row = jnp.where(lax.broadcasted_iota(jnp.int32, (16, BLOCK), 0) == 0, 1.0, 0.0)

    def blocks_of(y):
        pieces = []
        for z in range(side):
            pieces += [ga_ref[y, z], gb_ref[z, y]]
        feats = jnp.concatenate(pieces, axis=0)
        projected = project_t(weight_t, feats)
        return projected, scores_of(rows, projected)

    def run(weights_of, finish):
        def one_row(d, carry):
            acc[...] = jnp.zeros_like(acc)
            own = d_ref[d]

            def one_group(g, inner):
                slots = [g * GROUP + i for i in range(GROUP)]
                blocks = [src_ref[d, slot] for slot in slots]
                per_slot = [weights_of(d, slot, block, own) for slot, block in zip(slots, blocks)]
                for h in range(HEADS):
                    edge = jnp.concatenate([piece for one in per_slot for piece in one[h]], axis=0)
                    values = jnp.concatenate([vt[block, h] for block in blocks], axis=1)
                    acc[h] += jnp.dot(values, edge, preferred_element_type=F32)
                return inner

            lax.fori_loop(0, count_ref[d] // GROUP, one_group, 0)
            finish(d, own)
            return carry

        lax.fori_loop(0, dest, one_row, 0)

    def store(d, factor):
        denominators = []
        for h in range(HEADS):
            scaled = acc[h] * factor[h:h + 1, :]
            p_ref[d, pl.ds(h * HEAD_DIM, HEAD_DIM)] = scaled[:HEAD_DIM].astype(BF16)
            denominators.append(scaled[HEAD_DIM:HEAD_DIM + 1])
        denominators.append(jnp.zeros((16 - HEADS, BLOCK), F32))
        p_ref[d, pl.ds(HID, 16)] = jnp.concatenate(denominators, axis=0).astype(BF16)

    def direct(d, slot, block, own):
        words = bits_ref[d, slot]
        live = jnp.concatenate([jnp.right_shift(words, k) & 1 for k in range(8)], axis=0) != 0
        result = []
        for h in range(HEADS):
            raw = st[block, :, pl.ds(h, 1)] + own[h:h + 1, :]
            result.append([jnp.where(live, jnp.exp(leaky_relu(raw)), 0.0).astype(BF16)])
        return result

    def prepare_direct(y, carry):
        projected, score = blocks_of(y)
        for z in range(side):
            at = slice(z * BLOCK, (z + 1) * BLOCK)
            block = y * side + z
            for h in range(HEADS):
                values = projected[h * HEAD_DIM:(h + 1) * HEAD_DIM, at].astype(F32)
                vt[block, h] = jnp.concatenate([values, ones_row], axis=0).astype(BF16)
            st[block] = jnp.transpose(score[:, at])
        return carry

    lax.fori_loop(0, side, prepare_direct, 0)
    run(direct, lambda d, own: store(d, jnp.ones_like(own)))


def aggregate(side, block_src, block_count, block_bits, ga, gb, target_scores, weight, att_src):
    vmem = pl.BlockSpec(memory_space=pltpu.VMEM)
    smem = pl.BlockSpec(memory_space=pltpu.SMEM)
    dest = block_src.shape[0]
    sources = side * side
    return pl.pallas_call(
        functools.partial(aggregate_kernel, side),
        out_shape=jax.ShapeDtypeStruct((dest, SUM_ROWS, BLOCK), BF16),
        in_specs=[smem, smem, vmem, vmem, vmem, vmem, vmem, vmem],
        out_specs=vmem,
        scratch_shapes=[
            pltpu.VMEM((sources, HEADS, V_ROWS, BLOCK), BF16),
            pltpu.VMEM((sources, BLOCK, 8), F32),
            pltpu.VMEM((HEADS, V_ROWS, BLOCK), F32),
        ],
        compiler_params=pltpu.CompilerParams(vmem_limit_bytes=40 * 1024 * 1024),
        name="aggregate_edges",
    )(block_src, block_count, block_bits, ga, gb, target_scores, weight, att_src)


def combine_kernel(cols, p_ref, x_ref, w_ref, asrc_ref, adst_ref, bias_ref, out_ref, land, send, recv):
    r, c = lax.axis_index("rows"), lax.axis_index("cols")
    barrier = pltpu.get_barrier_semaphore()
    for k in range(1, cols):
        pl.semaphore_signal(barrier, inc=1, device_id=(r, (c + k) % cols), device_id_type=MESH)
    pl.semaphore_wait(barrier, cols - 1)
    copies = []
    for k in range(1, cols):
        peer = (c + k) % cols
        copies.append(pltpu.make_async_remote_copy(
            p_ref.at[peer], land.at[k - 1], send.at[k - 1], recv.at[k - 1],
            device_id=(r, peer), device_id_type=MESH))
        copies[-1].start()

    projected = project_t(transposed(w_ref[...]), x_ref[...])
    raw = scores_of(vector_rows(asrc_ref[...]), projected) + scores_of(vector_rows(adst_ref[...]), projected)
    self_weight = jnp.exp(leaky_relu(raw)).astype(BF16).astype(F32)
    own = p_ref[c].astype(F32)
    numerator = [
        own[h * HEAD_DIM:(h + 1) * HEAD_DIM]
        + projected[h * HEAD_DIM:(h + 1) * HEAD_DIM].astype(F32) * self_weight[h:h + 1]
        for h in range(HEADS)
    ]
    total = jnp.concatenate(numerator, axis=0)
    denominator = own[HID:HID + 8] + self_weight
    for k, copy in enumerate(copies):
        copy.wait_recv()
        total = total + land[k, pl.ds(0, HID)].astype(F32)
        denominator = denominator + land[k, pl.ds(HID, 16)].astype(F32)[:8]
    blended = jnp.concatenate(
        [total[h * HEAD_DIM:(h + 1) * HEAD_DIM] / denominator[h:h + 1] for h in range(HEADS)], axis=0)
    value = jnp.transpose(blended) + bias_ref[...]
    out_ref[...] = jnp.where(value > 0, value, jnp.exp(jnp.minimum(value, 0.0)) - 1.0).astype(BF16)
    for copy in copies:
        copy.wait_send()


def combine(cols, partials, node_feats, weight, att_src, att_dst, out_bias):
    vmem = pl.BlockSpec(memory_space=pltpu.VMEM)
    return pl.pallas_call(
        functools.partial(combine_kernel, cols),
        out_shape=jax.ShapeDtypeStruct((BLOCK, HID), BF16),
        in_specs=[vmem] * 6,
        out_specs=vmem,
        scratch_shapes=[
            pltpu.VMEM((cols - 1, SUM_ROWS, BLOCK), BF16),
            pltpu.SemaphoreType.DMA((cols - 1,)),
            pltpu.SemaphoreType.DMA((cols - 1,)),
        ],
        compiler_params=pltpu.CompilerParams(collective_id=2, has_side_effects=True),
        name="combine_partials",
    )(partials, node_feats, weight, att_src, att_dst, out_bias)


def direct_shards(side, cols, node_feats, weight, att_src, att_dst, out_bias, block_src, block_count, block_bits):
    att_src, att_dst, out_bias = (v.reshape(1, HID) for v in (att_src, att_dst, out_bias))
    ga, gb, target_scores = gather(side, cols, node_feats, weight, att_dst)
    partials = aggregate(
        side, block_src[0], block_count[0], block_bits[0], ga, gb, target_scores, weight, att_src)
    return combine(cols, partials, node_feats, weight, att_src, att_dst, out_bias)


def shards(side, cols, *args):
    node_feats, weight, att_src, att_dst, out_bias, block_src, block_count, block_bits = args
    result, peak = layer(
        side, cols, node_feats, weight, att_src.reshape(1, HID), att_dst.reshape(1, HID), out_bias.reshape(1, HID),
        block_src[0], block_count, block_bits[0])
    return lax.cond(peak[0, 0] <= SAFE, lambda *rest: result, functools.partial(direct_shards, side, cols), *args)


def solution(mesh):
    side = math.isqrt(mesh.shape["rows"])
    cols = mesh.shape["cols"]
    in_specs = (
        P(("rows", "cols"), None),
        P(),
        P(),
        P(),
        P(),
        P(("rows", "cols"), None, None),
        P(("rows", "cols"), None),
        P(("rows", "cols"), None, None, None, None),
    )
    return jax.shard_map(
        functools.partial(shards, side, cols), mesh=mesh, in_specs=in_specs,
        out_specs=P(("rows", "cols"), None), check_vma=False)
```

```python
import functools
import math

import jax
import jax.numpy as jnp
from jax import lax
from jax.experimental import pallas as pl
from jax.experimental.pallas import tpu as pltpu
from jax.sharding import PartitionSpec as P

HEADS = 4
BLOCK = 128
HEAD_DIM = 64
HID = HEADS * HEAD_DIM
SLOPE = 0.2
RISE = 1.0 - SLOPE
SAFE = 100.0
V_ROWS = 80
P_ROWS = HID + 16
OPEN = float(jnp.finfo(jnp.bfloat16).max)
HALF = BLOCK // 2
SUM_ROWS = HID + 16
GROUP = 4
MESH = pl.DeviceIdType.MESH
F32 = jnp.float32
BF16 = jnp.bfloat16
NT = (((1,), (1,)), ((), ()))


def leaky_relu(raw_score):
    return jnp.where(raw_score > 0, raw_score, SLOPE * raw_score)


def attention_rows(att_src, att_dst):
    row = lax.broadcasted_iota(jnp.int32, (32, HID), 0)
    column = lax.broadcasted_iota(jnp.int32, (32, HID), 1)
    att = jnp.where(row % 8 < HEADS, att_src, att_dst)
    high = att.astype(BF16).astype(F32)
    middle = (att - high).astype(BF16).astype(F32)
    low = att - high - middle
    piece = jnp.where(row < 8, high, jnp.where(row < 16, middle, low))
    return jnp.where((row % HEADS == column // HEAD_DIM) & (row < 24), piece, 0.0).astype(BF16)


def scores_of(rows, projected_t):
    parts = jnp.dot(rows, projected_t, preferred_element_type=F32)
    return parts[0:8] + parts[8:16] + parts[16:24]


def project_t(weight_t, feats):
    return lax.dot_general(weight_t, feats, NT, preferred_element_type=F32).astype(BF16)


def layer_kernel(side, cols, src_ref, count_ref, x_any, w_any, asrc_any, adst_any, bias_any, bits_any, out_ref, peak_ref,
                 x_ref, w_ref, asrc_ref, adst_ref, bias_ref, bits, feats, dme, dall, wt, rows, vt, eb, mask, parts, land,
                 own_total, own_weight, load_sem, d_send, d_recv, one_send, one_recv, two_send, two_recv, rs_send, rs_recv):
    r, c = lax.axis_index("rows"), lax.axis_index("cols")
    y, z = r // side, r % side
    quarter = side // 2
    links = bits.shape[1]

    def at(yy, zz):
        return (yy * side + zz, c)

    loads = [
        pltpu.make_async_copy(a, b, load_sem.at[i])
        for i, (a, b) in enumerate([
            (x_any, x_ref), (w_any, w_ref), (asrc_any, asrc_ref), (adst_any, adst_ref), (bias_any, bias_ref),
            (bits_any, bits)])
    ]
    for copy in loads:
        copy.start()

    barrier = pltpu.get_barrier_semaphore()
    for k in range(1, side):
        pl.semaphore_signal(barrier, inc=1, device_id=at(y, (z + k) % side), device_id_type=MESH)
        pl.semaphore_signal(barrier, inc=1, device_id=at((y + k) % side, z), device_id_type=MESH)
    for k in range(1, cols):
        pl.semaphore_signal(barrier, inc=1, device_id=(r, (c + k) % cols), device_id_type=MESH)

    for copy in loads[:4]:
        copy.wait()

    odd = (y + z) % 2
    block = jnp.where(odd == 0, y, z)
    index = jnp.where(odd == 0, z, y) // 2
    place = lax.broadcasted_iota(jnp.int32, (BLOCK, BLOCK), 0)
    node = lax.broadcasted_iota(jnp.int32, (BLOCK, BLOCK), 1)
    order = jnp.where(node == 8 * (place % 16) + place // 16, 1.0, 0.0).astype(BF16)
    feats[odd, block, index] = jnp.dot(order, x_ref[...], preferred_element_type=F32).astype(BF16)

    pl.semaphore_wait(barrier, 2 * (side - 1) + cols - 1)
    first = []
    for k in range(1, side):
        peer = at(jnp.where(odd == 0, y, (y + k) % side), jnp.where(odd == 0, (z + k) % side, z))
        mine = feats.at[odd, block, index]
        first.append(pltpu.make_async_remote_copy(
            mine, mine, one_send.at[k - 1], one_recv.at[k - 1], device_id=peer, device_id_type=MESH))
        first[-1].start()

    halves = (odd, 1 - odd)
    sent = {}

    def along(half, delta):
        target_y = jnp.where(half == 0, (y + delta + side) % side, y)
        target_z = jnp.where(half == 0, z, (z + delta + side) % side)
        return at(target_y, target_z)

    def pass_on(role, way, step, piece):
        half = halves[role]
        me, across = jnp.where(half == 0, y, z), jnp.where(half == 0, z, y)
        sign = 1 if way == 0 else -1
        origin = (me - sign * (step - 1) + side) % side
        same = (role + step - 1) % 2 == 0
        offset = ((0, 2, -2, 4) if same else (1, -1, 3, -3))[piece]
        ref = feats.at[half, origin, (across + offset + side) % side // 2]
        copy = pltpu.make_async_remote_copy(
            ref, ref, two_send.at[half, way, step - 1, piece], two_recv.at[half, way, step - 1, piece],
            device_id=along(half, sign), device_id_type=MESH)
        copy.start()
        sent[role, way, step, piece] = copy

    lanes = [(role, way) for role in range(2) for way in range(2)]

    def forward(step, pieces):
        for piece in pieces:
            for role, way in lanes:
                arrive(role, way, step - 1, piece)
                if step < side // 2 or piece // 2 == way:
                    pass_on(role, way, step, piece)

    def arrive(role, way, step, piece):
        sent[role, way, step, piece].wait_recv()

    for way in range(2):
        pass_on(0, way, 1, 0)

    wt[...] = jnp.transpose(w_ref[...].astype(F32)).astype(BF16)
    rows[...] = attention_rows(asrc_ref[...], adst_ref[...])
    projected = project_t(wt[...], x_ref[...])
    own_score = scores_of(rows[...], projected)
    dme[...] = jnp.concatenate([own_score[HEADS:], own_score[:HEADS]], axis=0)
    scores = []
    for k in range(1, cols):
        scores.append(pltpu.make_async_remote_copy(
            dme, dall.at[c], d_send.at[k - 1], d_recv.at[k - 1],
            device_id=(r, (c + k) % cols), device_id_type=MESH))
        scores[-1].start()
    dall[c] = dme[...]
    raw = own_score[:HEADS] + own_score[HEADS:]
    self_weight = jnp.exp(leaky_relu(raw)).astype(BF16).astype(F32)
    own_weight[...] = jnp.concatenate([self_weight, jnp.zeros_like(self_weight)], axis=0)
    own_total[...] = jnp.concatenate(
        [projected[h * HEAD_DIM:(h + 1) * HEAD_DIM].astype(F32) * self_weight[h:h + 1] for h in range(HEADS)], axis=0)

    for copy in loads[4:]:
        copy.wait()

    def unpack(i, carry):
        d, slot = i // links, i % links
        live = jnp.where(slot < count_ref[0, d], 1, 0)
        words = (bits[d, slot] * live).astype(jnp.int16)
        for k in range(8):
            mask[d, slot, pl.ds(16 * k, 16)] = jnp.where(
                (words & (1 << k)) != 0, jnp.asarray(OPEN, BF16), jnp.asarray(0.0, BF16))
        return carry

    def take(role, piece, distance):
        first[distance - 1].wait_recv()
        for way in range(2):
            pass_on(role, way, 1, piece)

    all_slots = bits.shape[0] * links
    lax.fori_loop(0, all_slots // 2, unpack, 0, unroll=4)
    take(1, 0, 7)
    take(1, 1, 1)
    lax.fori_loop(all_slots // 2, all_slots, unpack, 0, unroll=4)
    for role, piece, distance in ((0, 1, 6), (0, 2, 2), (1, 2, 5), (1, 3, 3), (0, 3, 4)):
        take(role, piece, distance)

    one_row = jnp.where(lax.broadcasted_iota(jnp.int32, (16, BLOCK), 0) == 0, 1.0, 0.0).astype(BF16)

    def prepare(half, where, largest):
        group = jnp.concatenate([feats[half, where, i] for i in range(quarter)], axis=0)
        values = project_t(wt[...], group)
        score = scores_of(rows[...], values)
        scale = jnp.exp(SLOPE * score).astype(BF16)
        rise = jnp.exp(RISE * score)
        for i in range(quarter):
            lane = slice(i * BLOCK, (i + 1) * BLOCK)
            across = 2 * i + (where + half) % 2
            source = jnp.where(half == 0, where * side + across, across * side + where)
            for h in range(HEADS):
                row = scale[h:h + 1, lane]
                vt[source, pl.ds(h * V_ROWS, HEAD_DIM)] = values[h * HEAD_DIM:(h + 1) * HEAD_DIM, lane] * row
                vt[source, pl.ds(h * V_ROWS + HEAD_DIM, 16)] = one_row * row
            column = jnp.transpose(rise[:, lane]).astype(BF16)
            for h in range(HEADS):
                eb[source, h] = jnp.broadcast_to(column[:, h:h + 1], (BLOCK, BLOCK))
        return jnp.maximum(largest, jnp.abs(score))

    def near(half, distance, largest):
        me = jnp.where(half == 0, y, z)
        largest = prepare(half, (me - distance + side) % side, largest)
        return prepare(half, (me + distance) % side, largest)

    largest = jnp.zeros((8, quarter * BLOCK), F32)
    forward(2, (0, 1))
    largest = prepare(0, y, largest)
    forward(2, (2,))
    largest = prepare(1, z, largest)
    forward(2, (3,))
    for step in (3, 4):
        distance = step - 2
        largest = prepare(0, (y - distance + side) % side, largest)
        forward(step, (0,))
        largest = prepare(0, (y + distance) % side, largest)
        forward(step, (1,))
        largest = prepare(1, (z - distance + side) % side, largest)
        forward(step, (2,))
        largest = prepare(1, (z + distance) % side, largest)
        forward(step, (3,))
    largest = lax.fori_loop(0, 2, lambda half, m: near(half, 3, m), largest)
    for role, way in lanes:
        for piece in (2 * way, 2 * way + 1):
            arrive(role, way, side // 2, piece)
    largest = prepare(0, (y + side // 2) % side, largest)
    largest = prepare(1, (z + side // 2) % side, largest)
    for copy in scores:
        copy.wait_recv()
    peak = jnp.broadcast_to(jnp.max(largest, axis=(0, 1), keepdims=True), (8, BLOCK))

    def send(k, d):
        return pltpu.make_async_remote_copy(
            parts.at[d], land.at[k - 1], rs_send.at[k - 1], rs_recv.at[k - 1], device_id=(r, d), device_id_type=MESH)

    def one_target(k, carry):
        d = (c + k) % cols
        target = dall[d]
        reach = jnp.exp(RISE * target).astype(BF16)
        fall = jnp.exp(SLOPE * target)
        sources = [src_ref[d, slot] for slot in range(links)]
        denominators = []
        for pair in range(HEADS // 2):
            weights = []
            for h in (2 * pair, 2 * pair + 1):
                mine = jnp.broadcast_to(reach[h:h + 1], (BLOCK, BLOCK))
                weights.append(jnp.concatenate([
                    jnp.minimum(jnp.maximum(eb[source, h] * mine, jnp.asarray(1.0, BF16)), mask[d, slot])
                    for slot, source in enumerate(sources)], axis=0))
            edge = jnp.concatenate(weights, axis=1)
            values = jnp.concatenate([vt[source, pl.ds(2 * pair * V_ROWS, 2 * V_ROWS)] for source in sources], axis=1)
            both = jnp.dot(values, edge, preferred_element_type=F32)
            for j in range(2):
                h = 2 * pair + j
                total = both[j * V_ROWS:(j + 1) * V_ROWS, j * BLOCK:(j + 1) * BLOCK] * fall[h:h + 1]
                parts[d, pl.ds(h * HEAD_DIM, HEAD_DIM)] = total[:HEAD_DIM].astype(BF16)
                denominators.append(total[HEAD_DIM:HEAD_DIM + 1])
        denominators += [jnp.zeros((8 - HEADS, BLOCK), F32), peak]
        parts[d, pl.ds(HID, 16)] = jnp.concatenate(denominators, axis=0).astype(BF16)

        @pl.when(k < cols)
        def _():
            send(k, d).start()

        return carry

    lax.fori_loop(1, cols + 1, one_target, 0)

    total = own_total[...] + parts[c, pl.ds(0, HID)].astype(F32)
    tail = parts[c, pl.ds(HID, 16)].astype(F32)
    denominator, peak = own_weight[...] + tail[:8], tail[8:]
    for k in range(1, cols):
        send(k, (c + k) % cols).wait_recv()
        total = total + land[k - 1, pl.ds(0, HID)].astype(F32)
        tail = land[k - 1, pl.ds(HID, 16)].astype(F32)
        denominator, peak = denominator + tail[:8], jnp.maximum(peak, tail[8:])
    blended = jnp.concatenate(
        [total[h * HEAD_DIM:(h + 1) * HEAD_DIM] / denominator[h:h + 1] for h in range(HEADS)], axis=0)
    value = jnp.transpose(blended) + bias_ref[...]
    out_ref[...] = jnp.where(value > 0, value, jnp.exp(jnp.minimum(value, 0.0)) - 1.0).astype(BF16)
    peak_ref[0, 0] = jnp.max(peak)
    for copy in first + scores + list(sent.values()):
        copy.wait_send()
    for k in range(1, cols):
        send(k, (c + k) % cols).wait_send()


def layer(side, cols, node_feats, weight, att_src, att_dst, out_bias, block_src, block_count, block_bits):
    vmem = pl.BlockSpec(memory_space=pltpu.VMEM)
    smem = pl.BlockSpec(memory_space=pltpu.SMEM)
    hbm = pl.BlockSpec(memory_space=pl.ANY)
    dma = pltpu.SemaphoreType.DMA
    sources = side * side
    dest, links = block_src.shape
    return pl.pallas_call(
        functools.partial(layer_kernel, side, cols),
        out_shape=(jax.ShapeDtypeStruct((BLOCK, HID), BF16), jax.ShapeDtypeStruct((1, 1), F32)),
        in_specs=[smem, smem] + [hbm] * 6,
        out_specs=(vmem, smem),
        scratch_shapes=[
            pltpu.VMEM((BLOCK, BLOCK), BF16),
            pltpu.VMEM((BLOCK, HID), BF16),
            pltpu.VMEM((1, HID), F32),
            pltpu.VMEM((1, HID), F32),
            pltpu.VMEM((1, HID), F32),
            pltpu.VMEM(block_bits.shape, jnp.int32),
            pltpu.VMEM((2, side, side // 2, BLOCK, BLOCK), BF16),
            pltpu.VMEM((8, BLOCK), F32),
            pltpu.VMEM((cols, 8, BLOCK), F32),
            pltpu.VMEM((HID, BLOCK), BF16),
            pltpu.VMEM((32, HID), BF16),
            pltpu.VMEM((sources, HEADS * V_ROWS, BLOCK), BF16),
            pltpu.VMEM((sources, HEADS, BLOCK, BLOCK), BF16),
            pltpu.VMEM((dest, links, BLOCK, BLOCK), BF16),
            pltpu.VMEM((cols, P_ROWS, BLOCK), BF16),
            pltpu.VMEM((cols - 1, P_ROWS, BLOCK), BF16),
            pltpu.VMEM((HID, BLOCK), F32),
            pltpu.VMEM((8, BLOCK), F32),
            dma((6,)), dma((cols - 1,)), dma((cols - 1,)), dma((side - 1,)), dma((side - 1,)),
            dma((2, 2, side // 2, side // 2)), dma((2, 2, side // 2, side // 2)), dma((cols - 1,)), dma((cols - 1,)),
        ],
        compiler_params=pltpu.CompilerParams(
            collective_id=0, has_side_effects=True, vmem_limit_bytes=56 * 1024 * 1024),
        name="attention_layer",
    )(block_src, block_count, node_feats, weight, att_src, att_dst, out_bias, block_bits)


def vector_rows(att):
    high = att.astype(BF16).astype(F32)
    middle = (att - high).astype(BF16).astype(F32)
    low = att - high - middle
    row = lax.broadcasted_iota(jnp.int32, (32, HID), 0)
    column = lax.broadcasted_iota(jnp.int32, (32, HID), 1)
    piece = jnp.where(row < 8, high, jnp.where(row < 16, middle, low))
    return jnp.where((row % 8 == column // HEAD_DIM) & (row < 24), piece, 0.0).astype(BF16)


def transposed(weight):
    return jnp.transpose(weight.astype(F32)).astype(BF16)


def gather_kernel(side, cols, x_ref, w_ref, adst_ref, ga_ref, gb_ref, d_ref, xp, dme,
                  local_sem, d_send, d_recv, one_send, one_recv, two_send, two_recv):
    r, c = lax.axis_index("rows"), lax.axis_index("cols")
    y, z = r // side, r % side

    def at(yy, zz):
        return (yy * side + zz, c)

    barrier = pltpu.get_barrier_semaphore()
    for k in range(1, side):
        pl.semaphore_signal(barrier, inc=1, device_id=at(y, (z + k) % side), device_id_type=MESH)
        pl.semaphore_signal(barrier, inc=1, device_id=at((y + k) % side, z), device_id_type=MESH)
    for k in range(1, cols):
        pl.semaphore_signal(barrier, inc=1, device_id=(r, (c + k) % cols), device_id_type=MESH)

    place = lax.broadcasted_iota(jnp.int32, (BLOCK, BLOCK), 0)
    node = lax.broadcasted_iota(jnp.int32, (BLOCK, BLOCK), 1)
    order = jnp.where(node == 8 * (place % 16) + place // 16, 1.0, 0.0).astype(BF16)
    xp[...] = jnp.dot(order, x_ref[...], preferred_element_type=F32).astype(BF16)
    dme[...] = scores_of(vector_rows(adst_ref[...]), project_t(transposed(w_ref[...]), x_ref[...]))
    pl.semaphore_wait(barrier, 2 * (side - 1) + cols - 1)

    first = []
    for k in range(1, side):
        first.append(pltpu.make_async_remote_copy(
            xp.at[pl.ds(0, HALF)], ga_ref.at[y, z], one_send.at[0, k - 1], one_recv.at[0, k - 1],
            device_id=at(y, (z + k) % side), device_id_type=MESH))
        first.append(pltpu.make_async_remote_copy(
            xp.at[pl.ds(HALF, HALF)], gb_ref.at[z, y], one_send.at[1, k - 1], one_recv.at[1, k - 1],
            device_id=at((y + k) % side, z), device_id_type=MESH))
    for copy in first:
        copy.start()
    own = [
        pltpu.make_async_copy(xp.at[pl.ds(0, HALF)], ga_ref.at[y, z], local_sem.at[0]),
        pltpu.make_async_copy(xp.at[pl.ds(HALF, HALF)], gb_ref.at[z, y], local_sem.at[1]),
        pltpu.make_async_copy(dme, d_ref.at[c], local_sem.at[2]),
    ]
    for copy in own:
        copy.start()
    scores = []
    for k in range(1, cols):
        scores.append(pltpu.make_async_remote_copy(
            dme, d_ref.at[c], d_send.at[k - 1], d_recv.at[k - 1],
            device_id=(r, (c + k) % cols), device_id_type=MESH))
        scores[-1].start()
    for copy in own:
        copy.wait()
    for copy in first:
        copy.wait_recv()

    sub = side // 2
    half_way = side // 2

    def second(half, way, step, part):
        buffer, place = (ga_ref, y) if half == 0 else (gb_ref, z)
        if way == 0:
            block, target = (place - step + 1 + side) % side, (place + 1) % side
        else:
            block, target = (place + step - 1) % side, (place + side - 1) % side
        ref = buffer.at[block, pl.ds(part * sub, sub)]
        return pltpu.make_async_remote_copy(
            ref, ref, two_send.at[half, way, step - 1, part], two_recv.at[half, way, step - 1, part],
            device_id=at(target, z) if half == 0 else at(y, target), device_id_type=MESH)

    lanes = [(half, way) for half in range(2) for way in range(2)]
    inflight = {}
    for step in range(1, half_way + 1):
        for part in range(2):
            for half, way in lanes:
                if step > 1:
                    inflight[half, way, step - 1, part].wait_recv()
                if step < half_way or part == way:
                    inflight[half, way, step, part] = second(half, way, step, part)
                    inflight[half, way, step, part].start()
    for half, way in lanes:
        inflight[half, way, half_way, way].wait_recv()
    for copy in scores:
        copy.wait_recv()
    for copy in first + scores + list(inflight.values()):
        copy.wait_send()


def gather(side, cols, node_feats, weight, att_dst):
    vmem = pl.BlockSpec(memory_space=pltpu.VMEM)
    hbm = pl.BlockSpec(memory_space=pl.ANY)
    dma = pltpu.SemaphoreType.DMA
    return pl.pallas_call(
        functools.partial(gather_kernel, side, cols),
        out_shape=(
            jax.ShapeDtypeStruct((side, side, HALF, BLOCK), BF16),
            jax.ShapeDtypeStruct((side, side, HALF, BLOCK), BF16),
            jax.ShapeDtypeStruct((cols, 8, BLOCK), F32),
        ),
        in_specs=[vmem, vmem, vmem],
        out_specs=(hbm, hbm, hbm),
        scratch_shapes=[
            pltpu.VMEM((BLOCK, BLOCK), BF16),
            pltpu.VMEM((8, BLOCK), F32),
            dma((3,)), dma((cols - 1,)), dma((cols - 1,)),
            dma((2, side - 1)), dma((2, side - 1)),
            dma((2, 2, side // 2, 2)), dma((2, 2, side // 2, 2)),
        ],
        compiler_params=pltpu.CompilerParams(collective_id=1, has_side_effects=True),
        name="gather_features",
    )(node_feats, weight, att_dst)


def aggregate_kernel(side, src_ref, count_ref, bits_ref, ga_ref, gb_ref, d_ref, w_ref, asrc_ref, p_ref,
                     vt, st, acc):
    dest = d_ref.shape[0]
    weight_t = transposed(w_ref[...])
    rows = vector_rows(asrc_ref[...])
    ones_row = jnp.where(lax.broadcasted_iota(jnp.int32, (16, BLOCK), 0) == 0, 1.0, 0.0)

    def blocks_of(y):
        pieces = []
        for z in range(side):
            pieces += [ga_ref[y, z], gb_ref[z, y]]
        feats = jnp.concatenate(pieces, axis=0)
        projected = project_t(weight_t, feats)
        return projected, scores_of(rows, projected)

    def run(weights_of, finish):
        def one_row(d, carry):
            acc[...] = jnp.zeros_like(acc)
            own = d_ref[d]

            def one_group(g, inner):
                slots = [g * GROUP + i for i in range(GROUP)]
                blocks = [src_ref[d, slot] for slot in slots]
                per_slot = [weights_of(d, slot, block, own) for slot, block in zip(slots, blocks)]
                for h in range(HEADS):
                    edge = jnp.concatenate([piece for one in per_slot for piece in one[h]], axis=0)
                    values = jnp.concatenate([vt[block, h] for block in blocks], axis=1)
                    acc[h] += jnp.dot(values, edge, preferred_element_type=F32)
                return inner

            lax.fori_loop(0, count_ref[d] // GROUP, one_group, 0)
            finish(d, own)
            return carry

        lax.fori_loop(0, dest, one_row, 0)

    def store(d, factor):
        denominators = []
        for h in range(HEADS):
            scaled = acc[h] * factor[h:h + 1, :]
            p_ref[d, pl.ds(h * HEAD_DIM, HEAD_DIM)] = scaled[:HEAD_DIM].astype(BF16)
            denominators.append(scaled[HEAD_DIM:HEAD_DIM + 1])
        denominators.append(jnp.zeros((16 - HEADS, BLOCK), F32))
        p_ref[d, pl.ds(HID, 16)] = jnp.concatenate(denominators, axis=0).astype(BF16)

    def direct(d, slot, block, own):
        words = bits_ref[d, slot]
        live = jnp.concatenate([jnp.right_shift(words, k) & 1 for k in range(8)], axis=0) != 0
        result = []
        for h in range(HEADS):
            raw = st[block, :, pl.ds(h, 1)] + own[h:h + 1, :]
            result.append([jnp.where(live, jnp.exp(leaky_relu(raw)), 0.0).astype(BF16)])
        return result

    def prepare_direct(y, carry):
        projected, score = blocks_of(y)
        for z in range(side):
            at = slice(z * BLOCK, (z + 1) * BLOCK)
            block = y * side + z
            for h in range(HEADS):
                values = projected[h * HEAD_DIM:(h + 1) * HEAD_DIM, at].astype(F32)
                vt[block, h] = jnp.concatenate([values, ones_row], axis=0).astype(BF16)
            st[block] = jnp.transpose(score[:, at])
        return carry

    lax.fori_loop(0, side, prepare_direct, 0)
    run(direct, lambda d, own: store(d, jnp.ones_like(own)))


def aggregate(side, block_src, block_count, block_bits, ga, gb, target_scores, weight, att_src):
    vmem = pl.BlockSpec(memory_space=pltpu.VMEM)
    smem = pl.BlockSpec(memory_space=pltpu.SMEM)
    dest = block_src.shape[0]
    sources = side * side
    return pl.pallas_call(
        functools.partial(aggregate_kernel, side),
        out_shape=jax.ShapeDtypeStruct((dest, SUM_ROWS, BLOCK), BF16),
        in_specs=[smem, smem, vmem, vmem, vmem, vmem, vmem, vmem],
        out_specs=vmem,
        scratch_shapes=[
            pltpu.VMEM((sources, HEADS, V_ROWS, BLOCK), BF16),
            pltpu.VMEM((sources, BLOCK, 8), F32),
            pltpu.VMEM((HEADS, V_ROWS, BLOCK), F32),
        ],
        compiler_params=pltpu.CompilerParams(vmem_limit_bytes=40 * 1024 * 1024),
        name="aggregate_edges",
    )(block_src, block_count, block_bits, ga, gb, target_scores, weight, att_src)


def combine_kernel(cols, p_ref, x_ref, w_ref, asrc_ref, adst_ref, bias_ref, out_ref, land, send, recv):
    r, c = lax.axis_index("rows"), lax.axis_index("cols")
    barrier = pltpu.get_barrier_semaphore()
    for k in range(1, cols):
        pl.semaphore_signal(barrier, inc=1, device_id=(r, (c + k) % cols), device_id_type=MESH)
    pl.semaphore_wait(barrier, cols - 1)
    copies = []
    for k in range(1, cols):
        peer = (c + k) % cols
        copies.append(pltpu.make_async_remote_copy(
            p_ref.at[peer], land.at[k - 1], send.at[k - 1], recv.at[k - 1],
            device_id=(r, peer), device_id_type=MESH))
        copies[-1].start()

    projected = project_t(transposed(w_ref[...]), x_ref[...])
    raw = scores_of(vector_rows(asrc_ref[...]), projected) + scores_of(vector_rows(adst_ref[...]), projected)
    self_weight = jnp.exp(leaky_relu(raw)).astype(BF16).astype(F32)
    own = p_ref[c].astype(F32)
    numerator = [
        own[h * HEAD_DIM:(h + 1) * HEAD_DIM]
        + projected[h * HEAD_DIM:(h + 1) * HEAD_DIM].astype(F32) * self_weight[h:h + 1]
        for h in range(HEADS)
    ]
    total = jnp.concatenate(numerator, axis=0)
    denominator = own[HID:HID + 8] + self_weight
    for k, copy in enumerate(copies):
        copy.wait_recv()
        total = total + land[k, pl.ds(0, HID)].astype(F32)
        denominator = denominator + land[k, pl.ds(HID, 16)].astype(F32)[:8]
    blended = jnp.concatenate(
        [total[h * HEAD_DIM:(h + 1) * HEAD_DIM] / denominator[h:h + 1] for h in range(HEADS)], axis=0)
    value = jnp.transpose(blended) + bias_ref[...]
    out_ref[...] = jnp.where(value > 0, value, jnp.exp(jnp.minimum(value, 0.0)) - 1.0).astype(BF16)
    for copy in copies:
        copy.wait_send()


def combine(cols, partials, node_feats, weight, att_src, att_dst, out_bias):
    vmem = pl.BlockSpec(memory_space=pltpu.VMEM)
    return pl.pallas_call(
        functools.partial(combine_kernel, cols),
        out_shape=jax.ShapeDtypeStruct((BLOCK, HID), BF16),
        in_specs=[vmem] * 6,
        out_specs=vmem,
        scratch_shapes=[
            pltpu.VMEM((cols - 1, SUM_ROWS, BLOCK), BF16),
            pltpu.SemaphoreType.DMA((cols - 1,)),
            pltpu.SemaphoreType.DMA((cols - 1,)),
        ],
        compiler_params=pltpu.CompilerParams(collective_id=2, has_side_effects=True),
        name="combine_partials",
    )(partials, node_feats, weight, att_src, att_dst, out_bias)


def direct_shards(side, cols, node_feats, weight, att_src, att_dst, out_bias, block_src, block_count, block_bits):
    att_src, att_dst, out_bias = (v.reshape(1, HID) for v in (att_src, att_dst, out_bias))
    ga, gb, target_scores = gather(side, cols, node_feats, weight, att_dst)
    partials = aggregate(
        side, block_src[0], block_count[0], block_bits[0], ga, gb, target_scores, weight, att_src)
    return combine(cols, partials, node_feats, weight, att_src, att_dst, out_bias)


def shards(side, cols, *args):
    node_feats, weight, att_src, att_dst, out_bias, block_src, block_count, block_bits = args
    result, peak = layer(
        side, cols, node_feats, weight, att_src.reshape(1, HID), att_dst.reshape(1, HID), out_bias.reshape(1, HID),
        block_src[0], block_count, block_bits[0])
    return lax.cond(peak[0, 0] <= SAFE, lambda *rest: result, functools.partial(direct_shards, side, cols), *args)


def solution(mesh):
    side = math.isqrt(mesh.shape["rows"])
    cols = mesh.shape["cols"]
    in_specs = (
        P(("rows", "cols"), None),
        P(),
        P(),
        P(),
        P(),
        P(("rows", "cols"), None, None),
        P(("rows", "cols"), None),
        P(("rows", "cols"), None, None, None, None),
    )
    return jax.shard_map(
        functools.partial(shards, side, cols), mesh=mesh, in_specs=in_specs,
        out_specs=P(("rows", "cols"), None), check_vma=False)
```
